128 devices in a mesh: station: 8 (over x, core), tm: 16 (over z, y).
Axes of the slice: x: 4, y: 4, z: 4, core: 2. Of those that a mesh axis runs over, the one named last changes fastest.
Arguments:
- voltages: bfloat16 [512, 512, 2, 1024], P('station', 'tm'), may hold values from -6 to 6
- taps: float32 [16, 1024], replicated, may hold values from -1.5 to 1.5
Outputs:
- visibilities: float32 [1024, 2, 512, 512], P(('station', 'tm'))
The draws below stay inside these ranges and needn't reach their ends.
All inputs are finite; a program needn't handle non-finite values.
Results may differ from the reference program's by a relative error of at most 0.0047.
Values may be sent and summed in bfloat16 or wider, within the bound.
No kernel may reach another device: no remote copies, remote signals or barrier semaphores. Data moves between devices by JAX's collectives and lax.ppermute only.
A program may use at most 192 MiB of HBM per device.

```python
import math
import jax
import jax.numpy as jnp
from jax import lax

INPUTS = 512
NFFT = 1024
TAPS = 16
SPECTRA = 512


def steps_of(own_key, extent, shards, low, top_value):
    factor_of = 1.0
    for dim, blocks in shards:
        heights = jax.random.uniform(jax.random.fold_in(jax.random.fold_in(own_key, 6), dim), (blocks,), jnp.float32, low / len(shards), top_value / len(shards))
        factor_of = factor_of * jnp.repeat(jnp.exp(heights), extent[dim] // blocks).reshape((-1,) + (1,) * (len(extent) - 1 - dim))
    return factor_of


def normal_values(key, extent, spread, most, shards=(), held_as=jnp.bfloat16):
    array = jax.random.normal(key, extent, jnp.float32) * spread
    if len(shards) > 0:
        array = steps_of(key, extent, shards, -0.22, 0.18) * array
    return jnp.clip(array, min=-most, max=most).astype(held_as)


def setup_inputs(seed: int = 0) -> dict:
    keys = jax.random.split(jax.random.key(seed), 3)
    return {
        "voltages": normal_values(keys[0], (INPUTS, SPECTRA, 2, NFFT), 1.0, 6.0, ((0, 8), (1, 16))),
        "taps": normal_values(keys[1], (TAPS, NFFT), TAPS ** -0.5, 1.5, (), jnp.float32),
    }


def dft_table(nfft):
    index = jnp.arange(nfft, dtype=jnp.int32)
    product = index[:, None] * index[None, :] % nfft
    angle = 2.0 * math.pi / nfft * product.astype(jnp.float32)
    cos_t = jnp.cos(angle) / math.sqrt(nfft)
    sin_t = jnp.sin(angle) / math.sqrt(nfft)
    upper = jnp.concatenate([cos_t, -sin_t], axis=1)
    lower = jnp.concatenate([sin_t, cos_t], axis=1)
    return jnp.concatenate([upper, lower], axis=0).astype(jnp.bfloat16)

def reference(voltages, taps):
    table = dft_table(NFFT)
    block_count = 8
    blocks = voltages.reshape(block_count, INPUTS // block_count, SPECTRA, 2, NFFT)

    def channelize(block):
        front = jnp.zeros((block.shape[0], TAPS - 1, 2, NFFT), block.dtype)
        padded = jnp.concatenate([front, block], axis=1)
        total = jnp.zeros(block.shape, jnp.float32)
        for k in range(TAPS):
            start = TAPS - 1 - k
            total = total + taps[k][None, None, None, :] * padded[:, start:start + SPECTRA].astype(jnp.float32)
        filtered = total.astype(jnp.bfloat16).reshape(-1, 2 * NFFT)
        spectra = jnp.dot(filtered, table, preferred_element_type=jnp.float32).astype(jnp.bfloat16)
        return spectra.reshape(block.shape)
    spectra = lax.map(channelize, blocks).reshape(INPUTS, SPECTRA, 2, NFFT)
    groups = NFFT // 8
    grouped = spectra.reshape(INPUTS, SPECTRA, 2, groups, 8).transpose(3, 4, 0, 2, 1)

    def correlate(group):
        left = group.reshape(8, INPUTS, 2 * SPECTRA).astype(jnp.float32)
        real_part = group[:, :, 0, :].astype(jnp.float32)
        imag_part = group[:, :, 1, :].astype(jnp.float32)
        twisted = jnp.concatenate([-imag_part, real_part], axis=-1)
        right = jnp.stack([left, twisted], axis=1)
        return jnp.einsum('cit,crjt->crij', left, right) * (1.0 / SPECTRA)
    result = lax.map(correlate, grouped)
    return result.reshape(NFFT, 2, INPUTS, INPUTS)
```

```python
import functools
import math

import jax
import jax.numpy as jnp
import ml_dtypes
import numpy as np
from jax import lax
from jax.experimental import pallas as pl
from jax.experimental.pallas import tpu as pltpu
from jax.sharding import PartitionSpec as P

AXES = ("station", "tm")
BEFORE = 8
INPUT_BLOCK = 16
PITCH = 24
EDGE_STEPS = 4
VMEM_BYTES = 60 * 1024 * 1024


def transform_rows(nfft):
    channel = np.arange(nfft, dtype=np.int64).reshape(nfft // 4, 4).T
    product = channel[:, :, None] * np.arange(nfft // 4, dtype=np.int64) % nfft
    angle = (np.float32(2.0 * math.pi / nfft) * product.astype(np.float32)).astype(np.float32)
    scale = np.float32(math.sqrt(nfft))
    parts = np.concatenate([np.cos(angle) / scale, np.sin(angle) / scale], axis=2)
    return parts.astype(ml_dtypes.bfloat16)


def filter_group(outputs, first, last, get, taps_ref, keep, wrap):
    tap_count = taps_ref.shape[0]
    own = [None] * len(outputs)
    for e in range(first, last):
        if wrap is not None and e == wrap:
            own = [a if f < wrap else a * keep for f, a in zip(outputs, own)]
        value = get(e).astype(jnp.float32)
        for n, f in enumerate(outputs):
            if 0 <= f - e < tap_count:
                term = taps_ref[f - e] * value
                own[n] = term if own[n] is None else own[n] + term
    return own


def channelize_body(groups, wrap, own_first, own_count, *refs):
    if wrap is None:
        taps_ref, table_ref, own_ref, out_ref, filtered, data, turned = refs
        keep = None
        before_ref = after_ref = None
    else:
        (keep_ref, taps_ref, table_ref, own_ref, before_ref, after_ref, out_ref, filtered, data, turned) = refs
        keep = keep_ref[0]
    step = pl.program_id(0)
    rows = INPUT_BLOCK

    def filter_input(i, _):
        def get(e):
            if e < own_first:
                return before_ref[i, e]
            if e < own_first + own_count:
                return own_ref[i, e - own_first]
            return after_ref[i, e - own_first - own_count]

        done = 0
        for outputs in groups:
            first = outputs[0] - (taps_ref.shape[0] - 1)
            values = filter_group(outputs, first, outputs[-1] + 1, get, taps_ref, keep, wrap)
            for n, value in enumerate(values):
                filtered[done + n, pl.ds(pl.multiple_of(i * PITCH, 8), 16), :] = value
            done += len(outputs)
        return 0

    lax.fori_loop(0, rows, filter_input, 0)

    def place(f, _):
        at = pl.ds(pl.multiple_of(step * rows, rows), rows)

        def sample(j):
            return [filtered[f, pl.ds(2 * j + part, rows, stride=PITCH), :] for part in range(2)]

        for q in range(2):
            z = [sample(q + 2 * m) for m in range(4)]
            even = [[a + b for a, b in zip(z[m], z[m + 2])] for m in range(2)]
            odd = [[a - b for a, b in zip(z[m], z[m + 2])] for m in range(2)]
            turned_odd = [odd[1][1], -odd[1][0]]
            folded = [
                [a + b for a, b in zip(even[0], even[1])],
                [a + b for a, b in zip(odd[0], turned_odd)],
                [a - b for a, b in zip(even[0], even[1])],
                [a - b for a, b in zip(odd[0], turned_odd)],
            ]
            low, high = pl.ds(q * 128, 128), pl.ds(256 + q * 128, 128)
            for p, (re, im) in enumerate(folded):
                re, im = re.astype(jnp.bfloat16), im.astype(jnp.bfloat16)
                data[p, f, 0, at, low] = re
                data[p, f, 0, at, high] = im
                data[p, f, 1, at, low] = im
                data[p, f, 1, at, high] = -re
        return 0

    lax.fori_loop(0, 16, place, 0)

    @pl.when(step == pl.num_programs(0) - 1)
    def _():
        def transform(n, _):
            for p in range(4):
                pair = data[p, pl.ds(2 * n, 2)].reshape(256, 512)
                result = lax.dot_general(
                    table_ref[p], pair, (((1,), (1,)), ((), ())), preferred_element_type=jnp.float32
                )
                turned[pl.ds(16 * p + 2 * n, 256, stride=64), :] = result[:, :128]
                turned[pl.ds(16 * p + 2 * n + 1, 256, stride=64), :] = result[:, 128:]
            return 0

        lax.fori_loop(0, 8, transform, 0)

        def write(d, _):
            block = turned[pl.ds(pl.multiple_of(d * 256, 256), 256), :]
            out_ref[pl.ds(2 * d, 2)] = block.reshape(2, 8, 16, 128).astype(jnp.bfloat16)
            return 0

        lax.fori_loop(0, 64, write, 0)


def channelize(groups, wrap, own_first, keep, taps, table, own, before, after, devices):
    inputs, own_count = own.shape[0], own.shape[1]
    whole = pl.BlockSpec(memory_space=pltpu.VMEM)

    def per_input(array):
        return pl.BlockSpec((INPUT_BLOCK,) + array.shape[1:], lambda s: (s, 0, 0, 0))

    operands, specs = [taps, table, own], [whole, whole, per_input(own)]
    if wrap is not None:
        operands = [keep] + operands + [before, after]
        specs = [pl.BlockSpec(memory_space=pltpu.SMEM)] + specs + [per_input(before), per_input(after)]
    return pl.pallas_call(
        functools.partial(channelize_body, groups, wrap, own_first, own_count),
        grid=(inputs // INPUT_BLOCK,),
        in_specs=specs,
        out_specs=whole,
        out_shape=jax.ShapeDtypeStruct((devices, 8, 16, 128), jnp.bfloat16),
        scratch_shapes=[
            pltpu.VMEM((16, INPUT_BLOCK * PITCH, 128), jnp.float32),
            pltpu.VMEM((4, 16, 2, 64, 512), jnp.bfloat16),
            pltpu.VMEM((1024 * 16, 128), jnp.float32),
        ],
        compiler_params=pltpu.CompilerParams(vmem_limit_bytes=VMEM_BYTES),
        cost_estimate=pl.CostEstimate(
            flops=64 * 1024 * 2048 * 2048, bytes_accessed=17 * 1024 * 1024, transcendentals=0
        ),
    )(*operands)


def edges_body(first_ref, last_ref, head_ref, tail_ref):
    head_ref[...] = first_ref[:, : head_ref.shape[1]]
    tail_ref[...] = last_ref[...]


def edges(own, head):
    inputs, frames = own.shape[:2]
    rows = inputs // EDGE_STEPS
    shapes = [(inputs, count) + own.shape[2:] for count in (head, BEFORE)]
    last = frames // BEFORE - 1
    return pl.pallas_call(
        edges_body,
        grid=(EDGE_STEPS,),
        in_specs=[
            pl.BlockSpec((rows, BEFORE) + own.shape[2:], lambda s: (s, 0, 0, 0)),
            pl.BlockSpec((rows, BEFORE) + own.shape[2:], lambda s: (s, last, 0, 0)),
        ],
        out_specs=[pl.BlockSpec((rows,) + shape[1:], lambda s: (s, 0, 0, 0)) for shape in shapes],
        out_shape=[jax.ShapeDtypeStruct(shape, own.dtype) for shape in shapes],
        compiler_params=pltpu.CompilerParams(vmem_limit_bytes=VMEM_BYTES),
    )(own, own)


def unpack_pair(low, high):
    real = jnp.concatenate([low[:, :64], high[:, :64]], axis=1)
    return real, jnp.concatenate([low[:, 64:], high[:, 64:]], axis=1)


def unpack_into(ref, store):
    for p in range(4):
        low = ref[pl.ds(32 * p, 16), 0].reshape(256, 128)
        high = ref[pl.ds(32 * p + 16, 16), 0].reshape(256, 128)
        store(pl.ds(128 * p, 128), *unpack_pair(low, high))


def received(spectra):
    return pl.BlockSpec((spectra.shape[0], 1, 16, 128), lambda c: (0, c, 0, 0))


def unpack_body(ref, out_ref):
    def store(at, real, imag):
        out_ref[0, 0, :, at] = real
        out_ref[0, 1, :, at] = imag

    unpack_into(ref, store)


def unpack(spectra):
    channels = spectra.shape[1]
    return pl.pallas_call(
        unpack_body,
        grid=(channels,),
        in_specs=[received(spectra)],
        out_specs=pl.BlockSpec((1, 2, 256, 512), lambda c: (c, 0, 0, 0)),
        out_shape=jax.ShapeDtypeStruct((channels, 2, 256, 512), jnp.bfloat16),
        compiler_params=pltpu.CompilerParams(vmem_limit_bytes=VMEM_BYTES),
        cost_estimate=pl.CostEstimate(
            flops=64 * 1024 * 2048 * 2048, bytes_accessed=9 * 1024 * 1024, transcendentals=0
        ),
    )(spectra)


def correlate_body(scale, ready_ref, ref, out_ref, real, imag):
    real[pl.ds(0, 256), :] = ready_ref[0, 0]
    imag[pl.ds(0, 256), :] = ready_ref[0, 1]

    def store(at, re, im):
        real[pl.ds(256, 256), at] = re
        imag[pl.ds(256, 256), at] = im

    unpack_into(ref, store)
    r, i = real[...], imag[...]
    rt, it = r.T, i.T

    def block(left, right, m, n):
        return jnp.dot(
            left[256 * m : 256 * m + 256], right[:, 256 * n : 256 * n + 256], preferred_element_type=jnp.float32
        )

    for m, n in ((0, 0), (0, 1), (1, 1)):
        rows, columns = pl.ds(256 * m, 256), pl.ds(256 * n, 256)
        value = (block(rt, r, m, n) + block(it, i, m, n)) * scale
        cross = block(it, r, m, n) * scale
        out_ref[0, 0, rows, columns] = value
        if m == n:
            out_ref[0, 1, rows, columns] = cross - cross.T
        else:
            cross = cross - block(rt, i, m, n) * scale
            out_ref[0, 0, columns, rows] = value.T
            out_ref[0, 1, rows, columns] = cross
            out_ref[0, 1, columns, rows] = -cross.T


def correlate(first, second, frames):
    channels = second.shape[1]
    return pl.pallas_call(
        functools.partial(correlate_body, 1.0 / frames),
        grid=(channels,),
        in_specs=[pl.BlockSpec((1, 2, 256, 512), lambda c: (c, 0, 0, 0)), received(second)],
        out_specs=pl.BlockSpec((1, 2, 512, 512), lambda c: (c, 0, 0, 0)),
        out_shape=jax.ShapeDtypeStruct((channels, 2, 512, 512), jnp.float32),
        scratch_shapes=[pltpu.VMEM((512, 512), jnp.bfloat16)] * 2,
        compiler_params=pltpu.CompilerParams(vmem_limit_bytes=VMEM_BYTES),
        cost_estimate=pl.CostEstimate(
            flops=16 * 512 * 512 * 1024, bytes_accessed=25 * 1024 * 1024, transcendentals=0
        ),
    )(first, second)


def per_device(voltages, taps):
    inputs, frames, _, nfft = voltages.shape
    tap_count = taps.shape[0]
    n_tm = lax.axis_size("tm")
    devices = n_tm * lax.axis_size("station")
    after_count = tap_count - 1 - BEFORE

    def blocked(a):
        return a.reshape(a.shape[0], a.shape[1], 2, 8, 128).transpose(0, 1, 3, 2, 4).reshape(a.shape[0], a.shape[1], 16, 128)

    own = blocked(voltages)
    up = [(d, d + 1) for d in range(n_tm - 1)]
    down = [(d, (d - 1) % n_tm) for d in range(n_tm)]
    head, tail = edges(own, after_count)
    before = lax.ppermute(tail, "tm", up)
    after = lax.ppermute(head, "tm", down)
    taps_rows = jnp.repeat(taps.reshape(tap_count, 8, 1, 128), 2, axis=2).reshape(tap_count, 16, 128)
    table = jnp.asarray(transform_rows(nfft))
    keep = (lax.axis_index("tm") < n_tm - 1).astype(jnp.float32).reshape(1)

    inner = [tuple(range(15, 23)), tuple(range(23, 31))]
    outer = [tuple(range(15, 23)), tuple(range(39, 47))]
    first = channelize(inner, None, 0, None, taps_rows, table, own, None, None, devices)
    first, after = lax.optimization_barrier((first, after))
    second = channelize(outer, BEFORE + frames, BEFORE, keep, taps_rows, table, own, before, after, devices)
    first = lax.all_to_all(first, AXES, 0, 0, tiled=True)
    second = lax.all_to_all(second, AXES, 0, 0, tiled=True)
    return correlate(unpack(first), second, n_tm * frames)


def solution(mesh):
    return jax.shard_map(
        per_device,
        mesh=mesh,
        in_specs=(P("station", "tm", None, None), P()),
        out_specs=P(("station", "tm"), None, None, None),
        check_vma=False,
    )
```

```python
import functools
import math

import jax
import jax.numpy as jnp
import ml_dtypes
import numpy as np
from jax import lax
from jax.experimental import pallas as pl
from jax.experimental.pallas import tpu as pltpu
from jax.sharding import PartitionSpec as P

AXES = ("station", "tm")
BEFORE = 8
INPUT_BLOCK = 16
PITCH = 24
EDGE_STEPS = 2
VMEM_BYTES = 60 * 1024 * 1024


def transform_rows(nfft):
    channel = np.arange(nfft, dtype=np.int64).reshape(nfft // 4, 4).T
    product = channel[:, :, None] * np.arange(nfft // 4, dtype=np.int64) % nfft
    angle = (np.float32(2.0 * math.pi / nfft) * product.astype(np.float32)).astype(np.float32)
    scale = np.float32(math.sqrt(nfft))
    parts = np.concatenate([np.cos(angle) / scale, np.sin(angle) / scale], axis=2)
    return parts.astype(ml_dtypes.bfloat16)


def filter_group(outputs, first, last, get, taps_ref, keep, wrap):
    tap_count = taps_ref.shape[0]
    own = [None] * len(outputs)
    for e in range(first, last):
        if wrap is not None and e == wrap:
            own = [a if f < wrap else a * keep for f, a in zip(outputs, own)]
        value = get(e).astype(jnp.float32)
        for n, f in enumerate(outputs):
            if 0 <= f - e < tap_count:
                term = taps_ref[f - e] * value
                own[n] = term if own[n] is None else own[n] + term
    return own


def channelize_body(groups, wrap, own_first, own_count, *refs):
    if wrap is None:
        taps_ref, table_ref, own_ref, out_ref, filtered, data, turned = refs
        keep = None
        before_ref = after_ref = None
    else:
        (keep_ref, taps_ref, table_ref, own_ref, before_ref, after_ref, out_ref, filtered, data, turned) = refs
        keep = keep_ref[0]
    step = pl.program_id(0)
    rows = INPUT_BLOCK

    def filter_input(i, _):
        def get(e):
            if e < own_first:
                return before_ref[i, e]
            if e < own_first + own_count:
                return own_ref[i, e - own_first]
            return after_ref[i, e - own_first - own_count]

        done = 0
        for outputs in groups:
            first = outputs[0] - (taps_ref.shape[0] - 1)
            values = filter_group(outputs, first, outputs[-1] + 1, get, taps_ref, keep, wrap)
            for n, value in enumerate(values):
                filtered[done + n, pl.ds(pl.multiple_of(i * PITCH, 8), 16), :] = value
            done += len(outputs)
        return 0

    lax.fori_loop(0, rows, filter_input, 0)

    def place(f, _):
        at = pl.ds(pl.multiple_of(step * rows, rows), rows)

        def sample(j):
            return [filtered[f, pl.ds(2 * j + part, rows, stride=PITCH), :] for part in range(2)]

        for q in range(2):
            z = [sample(q + 2 * m) for m in range(4)]
            even = [[a + b for a, b in zip(z[m], z[m + 2])] for m in range(2)]
            odd = [[a - b for a, b in zip(z[m], z[m + 2])] for m in range(2)]
            turned_odd = [odd[1][1], -odd[1][0]]
            folded = [
                [a + b for a, b in zip(even[0], even[1])],
                [a + b for a, b in zip(odd[0], turned_odd)],
                [a - b for a, b in zip(even[0], even[1])],
                [a - b for a, b in zip(odd[0], turned_odd)],
            ]
            low, high = pl.ds(q * 128, 128), pl.ds(256 + q * 128, 128)
            for p, (re, im) in enumerate(folded):
                re, im = re.astype(jnp.bfloat16), im.astype(jnp.bfloat16)
                data[p, f, 0, at, low] = re
                data[p, f, 0, at, high] = im
                data[p, f, 1, at, low] = im
                data[p, f, 1, at, high] = -re
        return 0

    lax.fori_loop(0, 16, place, 0)

    @pl.when(step == pl.num_programs(0) - 1)
    def _():
        def transform(n, _):
            for p in range(4):
                pair = data[p, pl.ds(2 * n, 2)].reshape(256, 512)
                result = lax.dot_general(
                    table_ref[p], pair, (((1,), (1,)), ((), ())), preferred_element_type=jnp.float32
                )
                turned[pl.ds(16 * p + 2 * n, 256, stride=64), :] = result[:, :128]
                turned[pl.ds(16 * p + 2 * n + 1, 256, stride=64), :] = result[:, 128:]
            return 0

        lax.fori_loop(0, 8, transform, 0)

        def write(d, _):
            block = turned[pl.ds(pl.multiple_of(d * 256, 256), 256), :]
            out_ref[pl.ds(2 * d, 2)] = block.reshape(2, 8, 16, 128).astype(jnp.bfloat16)
            return 0

        lax.fori_loop(0, 64, write, 0)


def channelize(groups, wrap, own_first, keep, taps, table, own, before, after, devices):
    inputs, own_count = own.shape[0], own.shape[1]
    whole = pl.BlockSpec(memory_space=pltpu.VMEM)

    def per_input(array):
        return pl.BlockSpec((INPUT_BLOCK,) + array.shape[1:], lambda s: (s, 0, 0, 0))

    operands, specs = [taps, table, own], [whole, whole, per_input(own)]
    if wrap is not None:
        operands = [keep] + operands + [before, after]
        specs = [pl.BlockSpec(memory_space=pltpu.SMEM)] + specs + [per_input(before), per_input(after)]
    return pl.pallas_call(
        functools.partial(channelize_body, groups, wrap, own_first, own_count),
        grid=(inputs // INPUT_BLOCK,),
        in_specs=specs,
        out_specs=whole,
        out_shape=jax.ShapeDtypeStruct((devices, 8, 16, 128), jnp.bfloat16),
        scratch_shapes=[
            pltpu.VMEM((16, INPUT_BLOCK * PITCH, 128), jnp.float32),
            pltpu.VMEM((4, 16, 2, 64, 512), jnp.bfloat16),
            pltpu.VMEM((1024 * 16, 128), jnp.float32),
        ],
        compiler_params=pltpu.CompilerParams(vmem_limit_bytes=VMEM_BYTES),
        cost_estimate=pl.CostEstimate(
            flops=64 * 1024 * 2048 * 2048, bytes_accessed=17 * 1024 * 1024, transcendentals=0
        ),
    )(*operands)


def edges_body(first_ref, last_ref, head_ref, tail_ref):
    head_ref[...] = first_ref[:, : head_ref.shape[1]]
    tail_ref[...] = last_ref[...]


def edges(own, head):
    inputs, frames = own.shape[:2]
    rows = inputs // EDGE_STEPS
    shapes = [(inputs, count) + own.shape[2:] for count in (head, BEFORE)]
    last = frames // BEFORE - 1
    return pl.pallas_call(
        edges_body,
        grid=(EDGE_STEPS,),
        in_specs=[
            pl.BlockSpec((rows, BEFORE) + own.shape[2:], lambda s: (s, 0, 0, 0)),
            pl.BlockSpec((rows, BEFORE) + own.shape[2:], lambda s: (s, last, 0, 0)),
        ],
        out_specs=[pl.BlockSpec((rows,) + shape[1:], lambda s: (s, 0, 0, 0)) for shape in shapes],
        out_shape=[jax.ShapeDtypeStruct(shape, own.dtype) for shape in shapes],
        compiler_params=pltpu.CompilerParams(vmem_limit_bytes=VMEM_BYTES),
    )(own, own)


def unpack_pair(low, high):
    real = jnp.concatenate([low[:, :64], high[:, :64]], axis=1)
    return real, jnp.concatenate([low[:, 64:], high[:, 64:]], axis=1)


def unpack_into(ref, store):
    for p in range(4):
        low = ref[pl.ds(32 * p, 16), 0].reshape(256, 128)
        high = ref[pl.ds(32 * p + 16, 16), 0].reshape(256, 128)
        store(pl.ds(128 * p, 128), *unpack_pair(low, high))


def received(spectra):
    return pl.BlockSpec((spectra.shape[0], 1, 16, 128), lambda c: (0, c, 0, 0))


def unpack_body(ref, out_ref):
    def store(at, real, imag):
        out_ref[0, 0, :, at] = real
        out_ref[0, 1, :, at] = imag

    unpack_into(ref, store)


def unpack(spectra):
    channels = spectra.shape[1]
    return pl.pallas_call(
        unpack_body,
        grid=(channels,),
        in_specs=[received(spectra)],
        out_specs=pl.BlockSpec((1, 2, 256, 512), lambda c: (c, 0, 0, 0)),
        out_shape=jax.ShapeDtypeStruct((channels, 2, 256, 512), jnp.bfloat16),
        compiler_params=pltpu.CompilerParams(vmem_limit_bytes=VMEM_BYTES),
        cost_estimate=pl.CostEstimate(
            flops=64 * 1024 * 2048 * 2048, bytes_accessed=9 * 1024 * 1024, transcendentals=0
        ),
    )(spectra)


def correlate_body(scale, ready_ref, ref, out_ref, real, imag):
    real[pl.ds(0, 256), :] = ready_ref[0, 0]
    imag[pl.ds(0, 256), :] = ready_ref[0, 1]

    def store(at, re, im):
        real[pl.ds(256, 256), at] = re
        imag[pl.ds(256, 256), at] = im

    unpack_into(ref, store)
    r, i = real[...], imag[...]
    rt, it = r.T, i.T

    def block(left, right, m, n):
        return jnp.dot(
            left[256 * m : 256 * m + 256], right[:, 256 * n : 256 * n + 256], preferred_element_type=jnp.float32
        )

    for m, n in ((0, 0), (0, 1), (1, 1)):
        rows, columns = pl.ds(256 * m, 256), pl.ds(256 * n, 256)
        value = (block(rt, r, m, n) + block(it, i, m, n)) * scale
        cross = block(it, r, m, n) * scale
        out_ref[0, 0, rows, columns] = value
        if m == n:
            out_ref[0, 1, rows, columns] = cross - cross.T
        else:
            cross = cross - block(rt, i, m, n) * scale
            out_ref[0, 0, columns, rows] = value.T
            out_ref[0, 1, rows, columns] = cross
            out_ref[0, 1, columns, rows] = -cross.T


def correlate(first, second, frames):
    channels = second.shape[1]
    return pl.pallas_call(
        functools.partial(correlate_body, 1.0 / frames),
        grid=(channels,),
        in_specs=[pl.BlockSpec((1, 2, 256, 512), lambda c: (c, 0, 0, 0)), received(second)],
        out_specs=pl.BlockSpec((1, 2, 512, 512), lambda c: (c, 0, 0, 0)),
        out_shape=jax.ShapeDtypeStruct((channels, 2, 512, 512), jnp.float32),
        scratch_shapes=[pltpu.VMEM((512, 512), jnp.bfloat16)] * 2,
        compiler_params=pltpu.CompilerParams(vmem_limit_bytes=VMEM_BYTES),
        cost_estimate=pl.CostEstimate(
            flops=16 * 512 * 512 * 1024, bytes_accessed=25 * 1024 * 1024, transcendentals=0
        ),
    )(first, second)


def per_device(voltages, taps):
    inputs, frames, _, nfft = voltages.shape
    tap_count = taps.shape[0]
    n_tm = lax.axis_size("tm")
    devices = n_tm * lax.axis_size("station")
    after_count = tap_count - 1 - BEFORE

    def blocked(a):
        return a.reshape(a.shape[0], a.shape[1], 2, 8, 128).transpose(0, 1, 3, 2, 4).reshape(a.shape[0], a.shape[1], 16, 128)

    own = blocked(voltages)
    up = [(d, d + 1) for d in range(n_tm - 1)]
    down = [(d, (d - 1) % n_tm) for d in range(n_tm)]
    head, tail = edges(own, after_count)
    before = lax.ppermute(tail, "tm", up)
    after = lax.ppermute(head, "tm", down)
    taps_rows = jnp.repeat(taps.reshape(tap_count, 8, 1, 128), 2, axis=2).reshape(tap_count, 16, 128)
    table = jnp.asarray(transform_rows(nfft))
    keep = (lax.axis_index("tm") < n_tm - 1).astype(jnp.float32).reshape(1)

    inner = [tuple(range(15, 23)), tuple(range(23, 31))]
    outer = [tuple(range(15, 23)), tuple(range(39, 47))]
    first = channelize(inner, None, 0, None, taps_rows, table, own, None, None, devices)
    first, before = lax.optimization_barrier((first, before))
    second = channelize(outer, BEFORE + frames, BEFORE, keep, taps_rows, table, own, before, after, devices)
    first = lax.all_to_all(first, AXES, 0, 0, tiled=True)
    second = lax.all_to_all(second, AXES, 0, 0, tiled=True)
    return correlate(unpack(first), second, n_tm * frames)


def solution(mesh):
    return jax.shard_map(
        per_device,
        mesh=mesh,
        in_specs=(P("station", "tm", None, None), P()),
        out_specs=P(("station", "tm"), None, None, None),
        check_vma=False,
    )
```

```python
import functools
import math

import jax
import jax.numpy as jnp
import ml_dtypes
import numpy as np
from jax import lax
from jax.experimental import pallas as pl
from jax.experimental.pallas import tpu as pltpu
from jax.sharding import PartitionSpec as P

AXES = ("station", "tm")
BEFORE = 8
INNER = tuple(range(23, 31)), tuple(range(31, 39))
OUTER = tuple(range(15, 23)), tuple(range(39, 47))
INPUT_BLOCK = 16
PITCH = 24
EDGE_STEPS = 2
VMEM_BYTES = 60 * 1024 * 1024


def transform_rows(nfft):
    channel = np.arange(nfft, dtype=np.int64).reshape(nfft // 4, 4).T
    product = channel[:, :, None] * np.arange(nfft // 4, dtype=np.int64) % nfft
    angle = (np.float32(2.0 * math.pi / nfft) * product.astype(np.float32)).astype(np.float32)
    scale = np.float32(math.sqrt(nfft))
    parts = np.concatenate([np.cos(angle) / scale, np.sin(angle) / scale], axis=2)
    return parts.astype(ml_dtypes.bfloat16)


def filter_terms(outputs, first, last, get, taps_ref, start):
    tap_count = taps_ref.shape[0]
    sums = list(start)
    for e in range(max(first, outputs[0] - tap_count + 1), min(last, outputs[-1] + 1)):
        value = get(e).astype(jnp.float32)
        for n, f in enumerate(outputs):
            if 0 <= f - e < tap_count:
                term = taps_ref[f - e] * value
                sums[n] = term if sums[n] is None else sums[n] + term
    return sums


def filter_own(i, wrap, keep, taps_ref, own_ref, partial_ref, filtered):
    def get(e):
        return own_ref[i, e - BEFORE]

    for g, outputs in enumerate(INNER):
        for n, value in enumerate(filter_terms(outputs, BEFORE, wrap, get, taps_ref, [None] * 8)):
            filtered[8 * g + n, pl.ds(pl.multiple_of(i * PITCH, 8), 16), :] = value
    for g, outputs in enumerate(OUTER):
        for n, value in enumerate(filter_terms(outputs, BEFORE, wrap, get, taps_ref, [None] * 8)):
            partial_ref[i, 8 * g + n] = value if outputs[n] < wrap else value * keep


def filter_halo(i, wrap, taps_ref, partial_ref, before_ref, after_ref, filtered):
    parts = (0, BEFORE, lambda e: before_ref[i, e]), (wrap, wrap + after_ref.shape[1], lambda e: after_ref[i, e - wrap])
    for g, (outputs, (first, last, get)) in enumerate(zip(OUTER, parts)):
        start = [partial_ref[i, 8 * g + n] for n in range(8)]
        for n, value in enumerate(filter_terms(outputs, first, last, get, taps_ref, start)):
            filtered[8 * g + n, pl.ds(pl.multiple_of(i * PITCH, 8), 16), :] = value


def channelize_body(wrap, halo, *refs):
    step = pl.program_id(0)
    rows = INPUT_BLOCK
    if halo:
        taps_ref, table_ref, partial_ref, before_ref, after_ref, out_ref, filtered, data, turned = refs
    else:
        keep_ref, taps_ref, table_ref, own_ref, out_ref, partial_ref, filtered, data, turned = refs

    def filter_input(i, _):
        if halo:
            filter_halo(i, wrap, taps_ref, partial_ref, before_ref, after_ref, filtered)
        else:
            filter_own(i, wrap, keep_ref[0], taps_ref, own_ref, partial_ref, filtered)
        return 0

    lax.fori_loop(0, rows, filter_input, 0)

    def place(f, _):
        at = pl.ds(pl.multiple_of(step * rows, rows), rows)

        def sample(j):
            return [filtered[f, pl.ds(2 * j + part, rows, stride=PITCH), :] for part in range(2)]

        for q in range(2):
            z = [sample(q + 2 * m) for m in range(4)]
            even = [[a + b for a, b in zip(z[m], z[m + 2])] for m in range(2)]
            odd = [[a - b for a, b in zip(z[m], z[m + 2])] for m in range(2)]
            turned_odd = [odd[1][1], -odd[1][0]]
            folded = [
                [a + b for a, b in zip(even[0], even[1])],
                [a + b for a, b in zip(odd[0], turned_odd)],
                [a - b for a, b in zip(even[0], even[1])],
                [a - b for a, b in zip(odd[0], turned_odd)],
            ]
            low, high = pl.ds(q * 128, 128), pl.ds(256 + q * 128, 128)
            for p, (re, im) in enumerate(folded):
                re, im = re.astype(jnp.bfloat16), im.astype(jnp.bfloat16)
                data[p, f, 0, at, low] = re
                data[p, f, 0, at, high] = im
                data[p, f, 1, at, low] = im
                data[p, f, 1, at, high] = -re
        return 0

    lax.fori_loop(0, 16, place, 0)

    @pl.when(step == pl.num_programs(0) - 1)
    def _():
        def transform(n, _):
            for p in range(4):
                pair = data[p, pl.ds(2 * n, 2)].reshape(256, 512)
                result = lax.dot_general(
                    table_ref[p], pair, (((1,), (1,)), ((), ())), preferred_element_type=jnp.float32
                )
                turned[pl.ds(16 * p + 2 * n, 256, stride=64), :] = result[:, :128]
                turned[pl.ds(16 * p + 2 * n + 1, 256, stride=64), :] = result[:, 128:]
            return 0

        lax.fori_loop(0, 8, transform, 0)

        def write(d, _):
            block = turned[pl.ds(pl.multiple_of(d * 256, 256), 256), :]
            out_ref[pl.ds(2 * d, 2)] = block.reshape(2, 8, 16, 128).astype(jnp.bfloat16)
            return 0

        lax.fori_loop(0, 64, write, 0)


def channelize(taps, table, devices, wrap, own=None, keep=None, partial=None, halo=()):
    inputs = (partial if own is None else own).shape[0]
    whole = pl.BlockSpec(memory_space=pltpu.VMEM)

    def per_input(shape):
        return pl.BlockSpec((INPUT_BLOCK,) + shape[1:], lambda s: (s, 0, 0, 0))

    sums = jax.ShapeDtypeStruct((inputs, 16, 16, 128), jnp.float32)
    blocks = jax.ShapeDtypeStruct((devices, 8, 16, 128), jnp.bfloat16)
    if own is None:
        operands = [taps, table, partial, *halo]
        specs = [whole, whole] + [per_input(a.shape) for a in operands[2:]]
        out_shape, out_specs = blocks, whole
    else:
        operands = [keep, taps, table, own]
        specs = [pl.BlockSpec(memory_space=pltpu.SMEM), whole, whole, per_input(own.shape)]
        out_shape, out_specs = [blocks, sums], [whole, per_input(sums.shape)]
    return pl.pallas_call(
        functools.partial(channelize_body, wrap, own is None),
        grid=(inputs // INPUT_BLOCK,),
        in_specs=specs,
        out_specs=out_specs,
        out_shape=out_shape,
        scratch_shapes=[
            pltpu.VMEM((16, INPUT_BLOCK * PITCH, 128), jnp.float32),
            pltpu.VMEM((4, 16, 2, 64, 512), jnp.bfloat16),
            pltpu.VMEM((1024 * 16, 128), jnp.float32),
        ],
        compiler_params=pltpu.CompilerParams(vmem_limit_bytes=VMEM_BYTES),
        cost_estimate=pl.CostEstimate(
            flops=64 * 1024 * 2048 * 2048, bytes_accessed=17 * 1024 * 1024, transcendentals=0
        ),
    )(*operands)


def edges_body(first_ref, last_ref, head_ref, tail_ref):
    head_ref[...] = first_ref[:, : head_ref.shape[1]]
    tail_ref[...] = last_ref[...]


def edges(own, head):
    inputs, frames = own.shape[:2]
    rows = inputs // EDGE_STEPS
    shapes = [(inputs, count) + own.shape[2:] for count in (head, BEFORE)]
    last = frames // BEFORE - 1
    return pl.pallas_call(
        edges_body,
        grid=(EDGE_STEPS,),
        in_specs=[
            pl.BlockSpec((rows, BEFORE) + own.shape[2:], lambda s: (s, 0, 0, 0)),
            pl.BlockSpec((rows, BEFORE) + own.shape[2:], lambda s: (s, last, 0, 0)),
        ],
        out_specs=[pl.BlockSpec((rows,) + shape[1:], lambda s: (s, 0, 0, 0)) for shape in shapes],
        out_shape=[jax.ShapeDtypeStruct(shape, own.dtype) for shape in shapes],
        compiler_params=pltpu.CompilerParams(vmem_limit_bytes=VMEM_BYTES),
    )(own, own)


def unpack_pair(low, high):
    real = jnp.concatenate([low[:, :64], high[:, :64]], axis=1)
    return real, jnp.concatenate([low[:, 64:], high[:, 64:]], axis=1)


def unpack_into(ref, store):
    for p in range(4):
        low = ref[pl.ds(32 * p, 16), 0].reshape(256, 128)
        high = ref[pl.ds(32 * p + 16, 16), 0].reshape(256, 128)
        store(pl.ds(128 * p, 128), *unpack_pair(low, high))


def received(spectra):
    return pl.BlockSpec((spectra.shape[0], 1, 16, 128), lambda c: (0, c, 0, 0))


def unpack_body(ref, out_ref):
    def store(at, real, imag):
        out_ref[0, 0, :, at] = real
        out_ref[0, 1, :, at] = imag

    unpack_into(ref, store)


def unpack(spectra):
    channels = spectra.shape[1]
    return pl.pallas_call(
        unpack_body,
        grid=(channels,),
        in_specs=[received(spectra)],
        out_specs=pl.BlockSpec((1, 2, 256, 512), lambda c: (c, 0, 0, 0)),
        out_shape=jax.ShapeDtypeStruct((channels, 2, 256, 512), jnp.bfloat16),
        compiler_params=pltpu.CompilerParams(vmem_limit_bytes=VMEM_BYTES),
        cost_estimate=pl.CostEstimate(
            flops=64 * 1024 * 2048 * 2048, bytes_accessed=9 * 1024 * 1024, transcendentals=0
        ),
    )(spectra)


def correlate_body(scale, ready_ref, ref, out_ref, real, imag):
    real[pl.ds(0, 256), :] = ready_ref[0, 0]
    imag[pl.ds(0, 256), :] = ready_ref[0, 1]

    def store(at, re, im):
        real[pl.ds(256, 256), at] = re
        imag[pl.ds(256, 256), at] = im

    unpack_into(ref, store)
    r, i = real[...], imag[...]
    rt, it = r.T, i.T

    def block(left, right, m, n):
        return jnp.dot(
            left[256 * m : 256 * m + 256], right[:, 256 * n : 256 * n + 256], preferred_element_type=jnp.float32
        )

    for m, n in ((0, 0), (0, 1), (1, 1)):
        rows, columns = pl.ds(256 * m, 256), pl.ds(256 * n, 256)
        value = (block(rt, r, m, n) + block(it, i, m, n)) * scale
        cross = block(it, r, m, n) * scale
        out_ref[0, 0, rows, columns] = value
        if m == n:
            out_ref[0, 1, rows, columns] = cross - cross.T
        else:
            cross = cross - block(rt, i, m, n) * scale
            out_ref[0, 0, columns, rows] = value.T
            out_ref[0, 1, rows, columns] = cross
            out_ref[0, 1, columns, rows] = -cross.T


def correlate(first, second, frames):
    channels = second.shape[1]
    return pl.pallas_call(
        functools.partial(correlate_body, 1.0 / frames),
        grid=(channels,),
        in_specs=[pl.BlockSpec((1, 2, 256, 512), lambda c: (c, 0, 0, 0)), received(second)],
        out_specs=pl.BlockSpec((1, 2, 512, 512), lambda c: (c, 0, 0, 0)),
        out_shape=jax.ShapeDtypeStruct((channels, 2, 512, 512), jnp.float32),
        scratch_shapes=[pltpu.VMEM((512, 512), jnp.bfloat16)] * 2,
        compiler_params=pltpu.CompilerParams(vmem_limit_bytes=VMEM_BYTES),
        cost_estimate=pl.CostEstimate(
            flops=16 * 512 * 512 * 1024, bytes_accessed=25 * 1024 * 1024, transcendentals=0
        ),
    )(first, second)


def per_device(voltages, taps):
    inputs, frames, _, nfft = voltages.shape
    tap_count = taps.shape[0]
    n_tm = lax.axis_size("tm")
    devices = n_tm * lax.axis_size("station")
    after_count = tap_count - 1 - BEFORE

    def blocked(a):
        return a.reshape(a.shape[0], a.shape[1], 2, 8, 128).transpose(0, 1, 3, 2, 4).reshape(a.shape[0], a.shape[1], 16, 128)

    own = blocked(voltages)
    up = [(d, d + 1) for d in range(n_tm - 1)]
    down = [(d, (d - 1) % n_tm) for d in range(n_tm)]
    head, tail = edges(own, after_count)
    before = lax.ppermute(tail, "tm", up)
    after = lax.ppermute(head, "tm", down)
    taps_rows = jnp.repeat(taps.reshape(tap_count, 8, 1, 128), 2, axis=2).reshape(tap_count, 16, 128)
    table = jnp.asarray(transform_rows(nfft))
    keep = (lax.axis_index("tm") < n_tm - 1).astype(jnp.float32).reshape(1)

    wrap = BEFORE + frames
    first, partial = channelize(taps_rows, table, devices, wrap, own=own, keep=keep)
    second = channelize(taps_rows, table, devices, wrap, partial=partial, halo=(before, after))
    first = lax.all_to_all(first, AXES, 0, 0, tiled=True)
    second = lax.all_to_all(second, AXES, 0, 0, tiled=True)
    return correlate(unpack(first), second, n_tm * frames)


def solution(mesh):
    return jax.shard_map(
        per_device,
        mesh=mesh,
        in_specs=(P("station", "tm", None, None), P()),
        out_specs=P(("station", "tm"), None, None, None),
        check_vma=False,
    )
```

```python
import functools
import math

import jax
import jax.numpy as jnp
import ml_dtypes
import numpy as np
from jax import lax
from jax.experimental import pallas as pl
from jax.experimental.pallas import tpu as pltpu
from jax.sharding import PartitionSpec as P

AXES = ("station", "tm")
BEFORE = 8
INNER = tuple(range(23, 31)), tuple(range(31, 39))
OUTER = tuple(range(15, 23)), tuple(range(39, 47))
INPUT_BLOCK = 16
PITCH = TURN = 24
EDGE_STEPS = 2
VMEM_BYTES = 60 * 1024 * 1024


def transform_rows(nfft):
    channel = np.arange(nfft, dtype=np.int64).reshape(nfft // 4, 4).T
    product = channel[:, :, None] * np.arange(nfft // 4, dtype=np.int64) % nfft
    angle = (np.float32(2.0 * math.pi / nfft) * product.astype(np.float32)).astype(np.float32)
    scale = np.float32(math.sqrt(nfft))
    parts = np.concatenate([np.cos(angle) / scale, np.sin(angle) / scale], axis=2)
    return parts.astype(ml_dtypes.bfloat16)


def filter_terms(outputs, first, last, get, taps_ref, start):
    tap_count = taps_ref.shape[0]
    sums = list(start)
    for e in range(max(first, outputs[0] - tap_count + 1), min(last, outputs[-1] + 1)):
        value = get(e).astype(jnp.float32)
        for n, f in enumerate(outputs):
            if 0 <= f - e < tap_count:
                term = taps_ref[f - e] * value
                sums[n] = term if sums[n] is None else sums[n] + term
    return sums


def filter_own(i, wrap, keep, taps_ref, own_ref, partial_ref, filtered):
    def get(e):
        return own_ref[i, e - BEFORE]

    for g, outputs in enumerate(INNER):
        for n, value in enumerate(filter_terms(outputs, BEFORE, wrap, get, taps_ref, [None] * 8)):
            filtered[8 * g + n, pl.ds(pl.multiple_of(i * PITCH, 8), 16), :] = value
    for g, outputs in enumerate(OUTER):
        for n, value in enumerate(filter_terms(outputs, BEFORE, wrap, get, taps_ref, [None] * 8)):
            partial_ref[i, 8 * g + n] = value if outputs[n] < wrap else value * keep


def filter_halo(i, wrap, taps_ref, partial_ref, before_ref, after_ref, filtered):
    parts = (0, BEFORE, lambda e: before_ref[i, e]), (wrap, wrap + after_ref.shape[1], lambda e: after_ref[i, e - wrap])
    for g, (outputs, (first, last, get)) in enumerate(zip(OUTER, parts)):
        start = [partial_ref[i, 8 * g + n] for n in range(8)]
        for n, value in enumerate(filter_terms(outputs, first, last, get, taps_ref, start)):
            filtered[8 * g + n, pl.ds(pl.multiple_of(i * PITCH, 8), 16), :] = value


def channelize_body(wrap, halo, *refs):
    step = pl.program_id(0)
    rows = INPUT_BLOCK
    if halo:
        taps_ref, table_ref, partial_ref, before_ref, after_ref, out_ref, filtered, data, turned = refs
    else:
        keep_ref, taps_ref, table_ref, own_ref, out_ref, partial_ref, filtered, data, turned = refs

    def filter_input(i, _):
        if halo:
            filter_halo(i, wrap, taps_ref, partial_ref, before_ref, after_ref, filtered)
        else:
            filter_own(i, wrap, keep_ref[0], taps_ref, own_ref, partial_ref, filtered)
        return 0

    lax.fori_loop(0, rows, filter_input, 0)

    def place(f, _):
        at = pl.ds(pl.multiple_of(step * rows, rows), rows)

        def sample(j):
            return [filtered[f, pl.ds(2 * j + part, rows, stride=PITCH), :] for part in range(2)]

        for q in range(2):
            z = [sample(q + 2 * m) for m in range(4)]
            even = [[a + b for a, b in zip(z[m], z[m + 2])] for m in range(2)]
            odd = [[a - b for a, b in zip(z[m], z[m + 2])] for m in range(2)]
            turned_odd = [odd[1][1], -odd[1][0]]
            folded = [
                [a + b for a, b in zip(even[0], even[1])],
                [a + b for a, b in zip(odd[0], turned_odd)],
                [a - b for a, b in zip(even[0], even[1])],
                [a - b for a, b in zip(odd[0], turned_odd)],
            ]
            low, high = pl.ds(q * 128, 128), pl.ds(256 + q * 128, 128)
            for p, (re, im) in enumerate(folded):
                re, im = re.astype(jnp.bfloat16), im.astype(jnp.bfloat16)
                data[p, f, 0, at, low] = re
                data[p, f, 0, at, high] = im
                data[p, f, 1, at, low] = im
                data[p, f, 1, at, high] = -re
        return 0

    lax.fori_loop(0, 16, place, 0)

    @pl.when(step == pl.num_programs(0) - 1)
    def _():
        def transform(n, _):
            for p in range(4):
                pair = data[p, pl.ds(2 * n, 2)].reshape(256, 512)
                result = lax.dot_general(
                    table_ref[p], pair, (((1,), (1,)), ((), ())), preferred_element_type=jnp.float32
                )
                turned[pl.ds(256 * TURN * p + 2 * n, 256, stride=TURN), :] = result[:, :128]
                turned[pl.ds(256 * TURN * p + 2 * n + 1, 256, stride=TURN), :] = result[:, 128:]
            return 0

        lax.fori_loop(0, 8, transform, 0)

        def write(d, _):
            for q in range(2):
                for p in range(4):
                    row = pl.multiple_of(2 * TURN * d, 8) + TURN * (256 * p + q)
                    out_ref[d, 4 * q + p] = turned[pl.ds(row, 16), :].astype(jnp.bfloat16)
            return 0

        lax.fori_loop(0, 128, write, 0, unroll=4)


def channelize(taps, table, devices, wrap, own=None, keep=None, partial=None, halo=()):
    inputs = (partial if own is None else own).shape[0]
    whole = pl.BlockSpec(memory_space=pltpu.VMEM)

    def per_input(shape):
        return pl.BlockSpec((INPUT_BLOCK,) + shape[1:], lambda s: (s, 0, 0, 0))

    sums = jax.ShapeDtypeStruct((inputs, 16, 16, 128), jnp.float32)
    blocks = jax.ShapeDtypeStruct((devices, 8, 16, 128), jnp.bfloat16)
    if own is None:
        operands = [taps, table, partial, *halo]
        specs = [whole, whole] + [per_input(a.shape) for a in operands[2:]]
        out_shape, out_specs = blocks, whole
    else:
        operands = [keep, taps, table, own]
        specs = [pl.BlockSpec(memory_space=pltpu.SMEM), whole, whole, per_input(own.shape)]
        out_shape, out_specs = [blocks, sums], [whole, per_input(sums.shape)]
    return pl.pallas_call(
        functools.partial(channelize_body, wrap, own is None),
        grid=(inputs // INPUT_BLOCK,),
        in_specs=specs,
        out_specs=out_specs,
        out_shape=out_shape,
        scratch_shapes=[
            pltpu.VMEM((16, INPUT_BLOCK * PITCH, 128), jnp.float32),
            pltpu.VMEM((4, 16, 2, 64, 512), jnp.bfloat16),
            pltpu.VMEM((1024 * TURN, 128), jnp.float32),
        ],
        compiler_params=pltpu.CompilerParams(vmem_limit_bytes=VMEM_BYTES),
        cost_estimate=pl.CostEstimate(
            flops=64 * 1024 * 2048 * 2048, bytes_accessed=17 * 1024 * 1024, transcendentals=0
        ),
    )(*operands)


def edge_body(first, source_ref, out_ref):
    out_ref[...] = source_ref[:, first : first + out_ref.shape[1]]


def edge(own, block, first, count):
    inputs = own.shape[0]
    rows = inputs // EDGE_STEPS
    return pl.pallas_call(
        functools.partial(edge_body, first),
        grid=(EDGE_STEPS,),
        in_specs=[pl.BlockSpec((rows, BEFORE) + own.shape[2:], lambda s: (s, block, 0, 0))],
        out_specs=pl.BlockSpec((rows, count) + own.shape[2:], lambda s: (s, 0, 0, 0)),
        out_shape=jax.ShapeDtypeStruct((inputs, count) + own.shape[2:], own.dtype),
        compiler_params=pltpu.CompilerParams(vmem_limit_bytes=VMEM_BYTES),
    )(own)


def unpack_pair(low, high):
    real = jnp.concatenate([low[:, :64], high[:, :64]], axis=1)
    return real, jnp.concatenate([low[:, 64:], high[:, 64:]], axis=1)


def unpack_into(ref, store):
    for p in range(4):
        low = ref[pl.ds(32 * p, 16), 0].reshape(256, 128)
        high = ref[pl.ds(32 * p + 16, 16), 0].reshape(256, 128)
        store(pl.ds(128 * p, 128), *unpack_pair(low, high))


def received(spectra):
    return pl.BlockSpec((spectra.shape[0], 1, 16, 128), lambda c: (0, c, 0, 0))


def unpack_body(ref, out_ref):
    def store(at, real, imag):
        out_ref[0, 0, :, at] = real
        out_ref[0, 1, :, at] = imag

    unpack_into(ref, store)


def unpack(spectra):
    channels = spectra.shape[1]
    return pl.pallas_call(
        unpack_body,
        grid=(channels,),
        in_specs=[received(spectra)],
        out_specs=pl.BlockSpec((1, 2, 256, 512), lambda c: (c, 0, 0, 0)),
        out_shape=jax.ShapeDtypeStruct((channels, 2, 256, 512), jnp.bfloat16),
        compiler_params=pltpu.CompilerParams(vmem_limit_bytes=VMEM_BYTES),
        cost_estimate=pl.CostEstimate(
            flops=64 * 1024 * 2048 * 2048, bytes_accessed=9 * 1024 * 1024, transcendentals=0
        ),
    )(spectra)


def correlate_body(scale, ready_ref, ref, out_ref, real, imag):
    real[pl.ds(0, 256), :] = ready_ref[0, 0]
    imag[pl.ds(0, 256), :] = ready_ref[0, 1]

    def store(at, re, im):
        real[pl.ds(256, 256), at] = re
        imag[pl.ds(256, 256), at] = im

    unpack_into(ref, store)
    r, i = real[...], imag[...]
    rt, it = r.T, i.T

    def block(left, right, m, n):
        return jnp.dot(
            left[256 * m : 256 * m + 256], right[:, 256 * n : 256 * n + 256], preferred_element_type=jnp.float32
        )

    for m, n in ((0, 0), (0, 1), (1, 1)):
        rows, columns = pl.ds(256 * m, 256), pl.ds(256 * n, 256)
        value = (block(rt, r, m, n) + block(it, i, m, n)) * scale
        cross = block(it, r, m, n) * scale
        out_ref[0, 0, rows, columns] = value
        if m == n:
            out_ref[0, 1, rows, columns] = cross - cross.T
        else:
            cross = cross - block(rt, i, m, n) * scale
            out_ref[0, 0, columns, rows] = value.T
            out_ref[0, 1, rows, columns] = cross
            out_ref[0, 1, columns, rows] = -cross.T


def correlate(first, second, frames):
    channels = second.shape[1]
    return pl.pallas_call(
        functools.partial(correlate_body, 1.0 / frames),
        grid=(channels,),
        in_specs=[pl.BlockSpec((1, 2, 256, 512), lambda c: (c, 0, 0, 0)), received(second)],
        out_specs=pl.BlockSpec((1, 2, 512, 512), lambda c: (c, 0, 0, 0)),
        out_shape=jax.ShapeDtypeStruct((channels, 2, 512, 512), jnp.float32),
        scratch_shapes=[pltpu.VMEM((512, 512), jnp.bfloat16)] * 2,
        compiler_params=pltpu.CompilerParams(vmem_limit_bytes=VMEM_BYTES),
        cost_estimate=pl.CostEstimate(
            flops=16 * 512 * 512 * 1024, bytes_accessed=25 * 1024 * 1024, transcendentals=0
        ),
    )(first, second)


def per_device(voltages, taps):
    inputs, frames, _, nfft = voltages.shape
    tap_count = taps.shape[0]
    n_tm = lax.axis_size("tm")
    devices = n_tm * lax.axis_size("station")
    after_count = tap_count - 1 - BEFORE

    def blocked(a):
        return a.reshape(a.shape[0], a.shape[1], 2, 8, 128).transpose(0, 1, 3, 2, 4).reshape(a.shape[0], a.shape[1], 16, 128)

    own = blocked(voltages)
    up = [(d, d + 1) for d in range(n_tm - 1)]
    down = [(d, (d - 1) % n_tm) for d in range(n_tm)]
    tail = edge(own, frames // BEFORE - 1, 0, BEFORE)
    before = lax.ppermute(tail, "tm", up)
    head = edge(lax.optimization_barrier((own, tail))[0], 0, 0, after_count)
    after = lax.ppermute(head, "tm", down)
    taps_rows = jnp.repeat(taps.reshape(tap_count, 8, 1, 128), 2, axis=2).reshape(tap_count, 16, 128)
    table = jnp.asarray(transform_rows(nfft))
    keep = (lax.axis_index("tm") < n_tm - 1).astype(jnp.float32).reshape(1)

    wrap = BEFORE + frames
    first, partial = channelize(taps_rows, table, devices, wrap, own=own, keep=keep)
    second = channelize(taps_rows, table, devices, wrap, partial=partial, halo=(before, after))
    first = lax.all_to_all(first, AXES, 0, 0, tiled=True)
    second = lax.all_to_all(second, AXES, 0, 0, tiled=True)
    return correlate(unpack(first), second, n_tm * frames)


def solution(mesh):
    return jax.shard_map(
        per_device,
        mesh=mesh,
        in_specs=(P("station", "tm", None, None), P()),
        out_specs=P(("station", "tm"), None, None, None),
        check_vma=False,
    )
```

```python
import functools
import math

import jax
import jax.numpy as jnp
import ml_dtypes
import numpy as np
from jax import lax
from jax.experimental import pallas as pl
from jax.experimental.pallas import tpu as pltpu
from jax.sharding import PartitionSpec as P

AXES = ("station", "tm")
BEFORE = 8
INNER = tuple(range(23, 31)), tuple(range(31, 39))
OUTER = tuple(range(15, 23)), tuple(range(39, 47))
INPUT_BLOCK = 16
PITCH = TURN = 24
EDGE_STEPS = 2
CHANNEL_BLOCK = 2
VMEM_BYTES = 60 * 1024 * 1024


def transform_rows(nfft):
    channel = np.arange(nfft, dtype=np.int64).reshape(nfft // 4, 4).T
    product = channel[:, :, None] * np.arange(nfft // 4, dtype=np.int64) % nfft
    angle = (np.float32(2.0 * math.pi / nfft) * product.astype(np.float32)).astype(np.float32)
    scale = np.float32(math.sqrt(nfft))
    parts = np.concatenate([np.cos(angle) / scale, np.sin(angle) / scale], axis=2)
    return parts.astype(ml_dtypes.bfloat16)


def filter_terms(outputs, first, last, get, taps_ref, start):
    tap_count = taps_ref.shape[0]
    sums = list(start)
    for e in range(max(first, outputs[0] - tap_count + 1), min(last, outputs[-1] + 1)):
        value = get(e).astype(jnp.float32)
        for n, f in enumerate(outputs):
            if 0 <= f - e < tap_count:
                term = taps_ref[f - e] * value
                sums[n] = term if sums[n] is None else sums[n] + term
    return sums


def filter_own(i, wrap, keep, taps_ref, own_ref, partial_ref, filtered):
    def get(e):
        return own_ref[i, e - BEFORE]

    for g, outputs in enumerate(INNER):
        for n, value in enumerate(filter_terms(outputs, BEFORE, wrap, get, taps_ref, [None] * 8)):
            filtered[8 * g + n, pl.ds(pl.multiple_of(i * PITCH, 8), 16), :] = value
    for g, outputs in enumerate(OUTER):
        for n, value in enumerate(filter_terms(outputs, BEFORE, wrap, get, taps_ref, [None] * 8)):
            partial_ref[i, 8 * g + n] = value if outputs[n] < wrap else value * keep


def filter_halo(i, wrap, taps_ref, partial_ref, before_ref, after_ref, filtered):
    parts = (0, BEFORE, lambda e: before_ref[i, e]), (wrap, wrap + after_ref.shape[1], lambda e: after_ref[i, e - wrap])
    for g, (outputs, (first, last, get)) in enumerate(zip(OUTER, parts)):
        start = [partial_ref[i, 8 * g + n] for n in range(8)]
        for n, value in enumerate(filter_terms(outputs, first, last, get, taps_ref, start)):
            filtered[8 * g + n, pl.ds(pl.multiple_of(i * PITCH, 8), 16), :] = value


def channelize_body(wrap, halo, *refs):
    step = pl.program_id(0)
    rows = INPUT_BLOCK
    if halo:
        taps_ref, table_ref, partial_ref, before_ref, after_ref, out_ref, filtered, data, turned = refs
    else:
        keep_ref, taps_ref, table_ref, own_ref, out_ref, partial_ref, filtered, data, turned = refs

    def filter_input(i, _):
        if halo:
            filter_halo(i, wrap, taps_ref, partial_ref, before_ref, after_ref, filtered)
        else:
            filter_own(i, wrap, keep_ref[0], taps_ref, own_ref, partial_ref, filtered)
        return 0

    lax.fori_loop(0, rows, filter_input, 0)

    def place(f, _):
        at = pl.ds(pl.multiple_of(step * rows, rows), rows)

        def sample(j):
            return [filtered[f, pl.ds(2 * j + part, rows, stride=PITCH), :] for part in range(2)]

        for q in range(2):
            z = [sample(q + 2 * m) for m in range(4)]
            even = [[a + b for a, b in zip(z[m], z[m + 2])] for m in range(2)]
            odd = [[a - b for a, b in zip(z[m], z[m + 2])] for m in range(2)]
            turned_odd = [odd[1][1], -odd[1][0]]
            folded = [
                [a + b for a, b in zip(even[0], even[1])],
                [a + b for a, b in zip(odd[0], turned_odd)],
                [a - b for a, b in zip(even[0], even[1])],
                [a - b for a, b in zip(odd[0], turned_odd)],
            ]
            low, high = pl.ds(q * 128, 128), pl.ds(256 + q * 128, 128)
            for p, (re, im) in enumerate(folded):
                re, im = re.astype(jnp.bfloat16), im.astype(jnp.bfloat16)
                data[p, f, 0, at, low] = re
                data[p, f, 0, at, high] = im
                data[p, f, 1, at, low] = im
                data[p, f, 1, at, high] = -re
        return 0

    lax.fori_loop(0, 16, place, 0)

    @pl.when(step == pl.num_programs(0) - 1)
    def _():
        def transform(n, _):
            for p in range(4):
                pair = data[p, pl.ds(2 * n, 2)].reshape(256, 512)
                result = lax.dot_general(
                    table_ref[p], pair, (((1,), (1,)), ((), ())), preferred_element_type=jnp.float32
                )
                turned[pl.ds(256 * TURN * p + 2 * n, 256, stride=TURN), :] = result[:, :128]
                turned[pl.ds(256 * TURN * p + 2 * n + 1, 256, stride=TURN), :] = result[:, 128:]
            return 0

        lax.fori_loop(0, 8, transform, 0)

        def write(d, _):
            for q in range(2):
                for p in range(4):
                    row = pl.multiple_of(2 * TURN * d, 8) + TURN * (256 * p + q)
                    out_ref[d, 4 * q + p] = turned[pl.ds(row, 16), :].astype(jnp.bfloat16)
            return 0

        lax.fori_loop(0, 128, write, 0, unroll=4)


def channelize(taps, table, devices, wrap, own=None, keep=None, partial=None, halo=()):
    inputs = (partial if own is None else own).shape[0]
    whole = pl.BlockSpec(memory_space=pltpu.VMEM)

    def per_input(shape):
        return pl.BlockSpec((INPUT_BLOCK,) + shape[1:], lambda s: (s, 0, 0, 0))

    sums = jax.ShapeDtypeStruct((inputs, 16, 16, 128), jnp.float32)
    blocks = jax.ShapeDtypeStruct((devices, 8, 16, 128), jnp.bfloat16)
    if own is None:
        operands = [taps, table, partial, *halo]
        specs = [whole, whole] + [per_input(a.shape) for a in operands[2:]]
        out_shape, out_specs = blocks, whole
    else:
        operands = [keep, taps, table, own]
        specs = [pl.BlockSpec(memory_space=pltpu.SMEM), whole, whole, per_input(own.shape)]
        out_shape, out_specs = [blocks, sums], [whole, per_input(sums.shape)]
    return pl.pallas_call(
        functools.partial(channelize_body, wrap, own is None),
        grid=(inputs // INPUT_BLOCK,),
        in_specs=specs,
        out_specs=out_specs,
        out_shape=out_shape,
        scratch_shapes=[
            pltpu.VMEM((16, INPUT_BLOCK * PITCH, 128), jnp.float32),
            pltpu.VMEM((4, 16, 2, 64, 512), jnp.bfloat16),
            pltpu.VMEM((1024 * TURN, 128), jnp.float32),
        ],
        compiler_params=pltpu.CompilerParams(vmem_limit_bytes=VMEM_BYTES),
        cost_estimate=pl.CostEstimate(
            flops=64 * 1024 * 2048 * 2048, bytes_accessed=17 * 1024 * 1024, transcendentals=0
        ),
    )(*operands)


def edge_body(first, source_ref, out_ref):
    out_ref[...] = source_ref[:, first : first + out_ref.shape[1]]


def edge(own, block, first, count):
    inputs = own.shape[0]
    rows = inputs // EDGE_STEPS
    return pl.pallas_call(
        functools.partial(edge_body, first),
        grid=(EDGE_STEPS,),
        in_specs=[pl.BlockSpec((rows, BEFORE) + own.shape[2:], lambda s: (s, block, 0, 0))],
        out_specs=pl.BlockSpec((rows, count) + own.shape[2:], lambda s: (s, 0, 0, 0)),
        out_shape=jax.ShapeDtypeStruct((inputs, count) + own.shape[2:], own.dtype),
        compiler_params=pltpu.CompilerParams(vmem_limit_bytes=VMEM_BYTES),
    )(own)


def unpack_pair(low, high):
    real = jnp.concatenate([low[:, :64], high[:, :64]], axis=1)
    return real, jnp.concatenate([low[:, 64:], high[:, 64:]], axis=1)


def unpacked(ref, channel):
    for p in range(4):
        low = ref[pl.ds(32 * p, 16), channel].reshape(256, 128)
        high = ref[pl.ds(32 * p + 16, 16), channel].reshape(256, 128)
        yield unpack_pair(low, high)


def received(spectra, channels):
    return pl.BlockSpec((spectra.shape[0], channels, 16, 128), lambda c: (0, c, 0, 0))


def unpack_body(ref, out_ref):
    for p, parts in enumerate(unpacked(ref, 0)):
        for n, part in enumerate(parts):
            out_ref[0, n, :, pl.ds(128 * p, 128)] = part


def unpack(spectra):
    channels = spectra.shape[1]
    return pl.pallas_call(
        unpack_body,
        grid=(channels,),
        in_specs=[received(spectra, 1)],
        out_specs=pl.BlockSpec((1, 2, 256, 512), lambda c: (c, 0, 0, 0)),
        out_shape=jax.ShapeDtypeStruct((channels, 2, 256, 512), jnp.bfloat16),
        compiler_params=pltpu.CompilerParams(vmem_limit_bytes=VMEM_BYTES),
        cost_estimate=pl.CostEstimate(
            flops=64 * 1024 * 2048 * 2048, bytes_accessed=9 * 1024 * 1024, transcendentals=0
        ),
    )(spectra)


def correlate_channel(scale, channel, ready_ref, ref, out_ref):
    arrived = [jnp.concatenate(blocks, axis=1) for blocks in zip(*unpacked(ref, channel))]
    r, i = [jnp.concatenate([ready_ref[channel, n], part], axis=0) for n, part in enumerate(arrived)]
    rt, it = r.T, i.T
    both_t, both = jnp.concatenate([rt, it], axis=1), jnp.concatenate([r, i], axis=0)

    def block(left, right, m, n):
        return jnp.dot(
            left[256 * m : 256 * m + 256], right[:, 256 * n : 256 * n + 256], preferred_element_type=jnp.float32
        )

    for m, n in ((0, 0), (0, 1), (1, 1)):
        rows, columns = pl.ds(256 * m, 256), pl.ds(256 * n, 256)
        value = block(both_t, both, m, n) * scale
        cross = block(it, r, m, n) * scale
        out_ref[channel, 0, rows, columns] = value
        if m == n:
            out_ref[channel, 1, rows, columns] = cross - cross.T
        else:
            cross = cross - block(rt, i, m, n) * scale
            out_ref[channel, 0, columns, rows] = value.T
            out_ref[channel, 1, rows, columns] = cross
            out_ref[channel, 1, columns, rows] = -cross.T


def correlate_body(scale, *refs):
    for channel in range(CHANNEL_BLOCK):
        correlate_channel(scale, channel, *refs)


def correlate(first, second, frames):
    channels = second.shape[1]
    return pl.pallas_call(
        functools.partial(correlate_body, 1.0 / frames),
        grid=(channels // CHANNEL_BLOCK,),
        in_specs=[pl.BlockSpec((CHANNEL_BLOCK, 2, 256, 512), lambda c: (c, 0, 0, 0)), received(second, CHANNEL_BLOCK)],
        out_specs=pl.BlockSpec((CHANNEL_BLOCK, 2, 512, 512), lambda c: (c, 0, 0, 0)),
        out_shape=jax.ShapeDtypeStruct((channels, 2, 512, 512), jnp.float32),
        compiler_params=pltpu.CompilerParams(vmem_limit_bytes=VMEM_BYTES),
        cost_estimate=pl.CostEstimate(
            flops=16 * 512 * 512 * 1024, bytes_accessed=25 * 1024 * 1024, transcendentals=0
        ),
    )(first, second)


def per_device(voltages, taps):
    inputs, frames, _, nfft = voltages.shape
    tap_count = taps.shape[0]
    n_tm = lax.axis_size("tm")
    devices = n_tm * lax.axis_size("station")
    after_count = tap_count - 1 - BEFORE

    def blocked(a):
        return a.reshape(a.shape[0], a.shape[1], 2, 8, 128).transpose(0, 1, 3, 2, 4).reshape(a.shape[0], a.shape[1], 16, 128)

    own = blocked(voltages)
    up = [(d, d + 1) for d in range(n_tm - 1)]
    down = [(d, (d - 1) % n_tm) for d in range(n_tm)]
    tail = edge(own, frames // BEFORE - 1, 0, BEFORE)
    before = lax.ppermute(tail, "tm", up)
    head = edge(lax.optimization_barrier((own, tail))[0], 0, 0, after_count)
    after = lax.ppermute(head, "tm", down)
    taps_rows = jnp.repeat(taps.reshape(tap_count, 8, 1, 128), 2, axis=2).reshape(tap_count, 16, 128)
    table = jnp.asarray(transform_rows(nfft))
    keep = (lax.axis_index("tm") < n_tm - 1).astype(jnp.float32).reshape(1)

    wrap = BEFORE + frames
    first, partial = channelize(taps_rows, table, devices, wrap, own=own, keep=keep)
    second = channelize(taps_rows, table, devices, wrap, partial=partial, halo=(before, after))
    first = lax.all_to_all(first, AXES, 0, 0, tiled=True)
    second = lax.all_to_all(second, AXES, 0, 0, tiled=True)
    return correlate(unpack(first), second, n_tm * frames)


def solution(mesh):
    return jax.shard_map(
        per_device,
        mesh=mesh,
        in_specs=(P("station", "tm", None, None), P()),
        out_specs=P(("station", "tm"), None, None, None),
        check_vma=False,
    )
```

```python
import functools
import math

import jax
import jax.numpy as jnp
import ml_dtypes
import numpy as np
from jax import lax
from jax.experimental import pallas as pl
from jax.experimental.pallas import tpu as pltpu
from jax.sharding import PartitionSpec as P

AXES = ("station", "tm")
BEFORE = 8
INNER = tuple(range(23, 31)), tuple(range(31, 39))
OUTER = tuple(range(15, 23)), tuple(range(39, 47))
INPUT_BLOCK = 16
PITCH = TURN = 24
EDGE_STEPS = 2
CHANNEL_BLOCK = 2
VMEM_BYTES = 60 * 1024 * 1024


def transform_rows(nfft):
    channel = np.arange(nfft, dtype=np.int64).reshape(nfft // 4, 4).T
    product = channel[:, :, None] * np.arange(nfft // 4, dtype=np.int64) % nfft
    angle = (np.float32(2.0 * math.pi / nfft) * product.astype(np.float32)).astype(np.float32)
    scale = np.float32(math.sqrt(nfft))
    parts = np.concatenate([np.cos(angle) / scale, np.sin(angle) / scale], axis=2)
    return parts.astype(ml_dtypes.bfloat16)


def filter_terms(outputs, first, last, get, taps_ref, start):
    tap_count = taps_ref.shape[0]
    sums = list(start)
    for e in range(max(first, outputs[0] - tap_count + 1), min(last, outputs[-1] + 1)):
        value = get(e).astype(jnp.float32)
        for n, f in enumerate(outputs):
            if 0 <= f - e < tap_count:
                term = taps_ref[f - e] * value
                sums[n] = term if sums[n] is None else sums[n] + term
    return sums


def filter_own(i, wrap, keep, taps_ref, own_ref, partial_ref, filtered):
    def get(e):
        return own_ref[i, e - BEFORE]

    for g, outputs in enumerate(INNER):
        for n, value in enumerate(filter_terms(outputs, BEFORE, wrap, get, taps_ref, [None] * 8)):
            filtered[8 * g + n, pl.ds(pl.multiple_of(i * PITCH, 8), 16), :] = value
    for g, outputs in enumerate(OUTER):
        for n, value in enumerate(filter_terms(outputs, BEFORE, wrap, get, taps_ref, [None] * 8)):
            partial_ref[i, 8 * g + n] = value if outputs[n] < wrap else value * keep


def filter_halo(i, wrap, taps_ref, partial_ref, before_ref, after_ref, filtered):
    parts = (0, BEFORE, lambda e: before_ref[i, e]), (wrap, wrap + after_ref.shape[1], lambda e: after_ref[i, e - wrap])
    for g, (outputs, (first, last, get)) in enumerate(zip(OUTER, parts)):
        start = [partial_ref[i, 8 * g + n] for n in range(8)]
        for n, value in enumerate(filter_terms(outputs, first, last, get, taps_ref, start)):
            filtered[8 * g + n, pl.ds(pl.multiple_of(i * PITCH, 8), 16), :] = value


def channelize_body(wrap, halo, *refs):
    step = pl.program_id(0)
    rows = INPUT_BLOCK
    if halo:
        taps_ref, table_ref, partial_ref, before_ref, after_ref, out_ref, filtered, data, turned, taps_rows = refs
    else:
        keep_ref, taps_ref, table_ref, own_ref, out_ref, partial_ref, filtered, data, turned, taps_rows = refs

    @pl.when(step == 0)
    def _():
        for j in range(8):
            block = taps_ref[:, 128 * j : 128 * j + 128]
            for part in range(2):
                taps_rows[:, 2 * j + part, :] = block

    def filter_input(i, _):
        if halo:
            filter_halo(i, wrap, taps_rows, partial_ref, before_ref, after_ref, filtered)
        else:
            filter_own(i, wrap, keep_ref[0], taps_rows, own_ref, partial_ref, filtered)
        return 0

    lax.fori_loop(0, rows, filter_input, 0)

    def place(f, _):
        at = pl.ds(pl.multiple_of(step * rows, rows), rows)

        def sample(j):
            return [filtered[f, pl.ds(2 * j + part, rows, stride=PITCH), :] for part in range(2)]

        for q in range(2):
            z = [sample(q + 2 * m) for m in range(4)]
            even = [[a + b for a, b in zip(z[m], z[m + 2])] for m in range(2)]
            odd = [[a - b for a, b in zip(z[m], z[m + 2])] for m in range(2)]
            turned_odd = [odd[1][1], -odd[1][0]]
            folded = [
                [a + b for a, b in zip(even[0], even[1])],
                [a + b for a, b in zip(odd[0], turned_odd)],
                [a - b for a, b in zip(even[0], even[1])],
                [a - b for a, b in zip(odd[0], turned_odd)],
            ]
            low, high = pl.ds(q * 128, 128), pl.ds(256 + q * 128, 128)
            for p, (re, im) in enumerate(folded):
                re, im = re.astype(jnp.bfloat16), im.astype(jnp.bfloat16)
                data[p, f, 0, at, low] = re
                data[p, f, 0, at, high] = im
                data[p, f, 1, at, low] = im
                data[p, f, 1, at, high] = -re
        return 0

    lax.fori_loop(0, 16, place, 0)

    @pl.when(step == pl.num_programs(0) - 1)
    def _():
        def transform(n, _):
            for p in range(4):
                pair = data[p, pl.ds(2 * n, 2)].reshape(256, 512)
                result = lax.dot_general(
                    table_ref[p], pair, (((1,), (1,)), ((), ())), preferred_element_type=jnp.float32
                )
                turned[pl.ds(256 * TURN * p + 2 * n, 256, stride=TURN), :] = result[:, :128]
                turned[pl.ds(256 * TURN * p + 2 * n + 1, 256, stride=TURN), :] = result[:, 128:]
            return 0

        lax.fori_loop(0, 8, transform, 0, unroll=2)

        def write(d, _):
            for q in range(2):
                for p in range(4):
                    row = pl.multiple_of(2 * TURN * d, 8) + TURN * (256 * p + q)
                    out_ref[d, 4 * q + p] = turned[pl.ds(row, 16), :].astype(jnp.bfloat16)
            return 0

        lax.fori_loop(0, 128, write, 0, unroll=4)


def channelize(taps, table, devices, wrap, own=None, keep=None, partial=None, halo=()):
    inputs = (partial if own is None else own).shape[0]
    whole = pl.BlockSpec(memory_space=pltpu.VMEM)

    def per_input(shape):
        return pl.BlockSpec((INPUT_BLOCK,) + shape[1:], lambda s: (s, 0, 0, 0))

    sums = jax.ShapeDtypeStruct((inputs, 16, 16, 128), jnp.float32)
    blocks = jax.ShapeDtypeStruct((devices, 8, 16, 128), jnp.bfloat16)
    if own is None:
        operands = [taps, table, partial, *halo]
        specs = [whole, whole] + [per_input(a.shape) for a in operands[2:]]
        out_shape, out_specs = blocks, whole
    else:
        operands = [keep, taps, table, own]
        specs = [pl.BlockSpec(memory_space=pltpu.SMEM), whole, whole, per_input(own.shape)]
        out_shape, out_specs = [blocks, sums], [whole, per_input(sums.shape)]
    return pl.pallas_call(
        functools.partial(channelize_body, wrap, own is None),
        grid=(inputs // INPUT_BLOCK,),
        in_specs=specs,
        out_specs=out_specs,
        out_shape=out_shape,
        scratch_shapes=[
            pltpu.VMEM((16, INPUT_BLOCK * PITCH, 128), jnp.float32),
            pltpu.VMEM((4, 16, 2, 64, 512), jnp.bfloat16),
            pltpu.VMEM((1024 * TURN, 128), jnp.float32),
            pltpu.VMEM((taps.shape[0], 16, 128), jnp.float32),
        ],
        compiler_params=pltpu.CompilerParams(vmem_limit_bytes=VMEM_BYTES),
        cost_estimate=pl.CostEstimate(
            flops=64 * 1024 * 2048 * 2048, bytes_accessed=17 * 1024 * 1024, transcendentals=0
        ),
    )(*operands)


def edge_body(first, source_ref, out_ref):
    out_ref[...] = source_ref[:, first : first + out_ref.shape[1]]


def edge(own, block, first, count):
    inputs = own.shape[0]
    rows = inputs // EDGE_STEPS
    return pl.pallas_call(
        functools.partial(edge_body, first),
        grid=(EDGE_STEPS,),
        in_specs=[pl.BlockSpec((rows, BEFORE) + own.shape[2:], lambda s: (s, block, 0, 0))],
        out_specs=pl.BlockSpec((rows, count) + own.shape[2:], lambda s: (s, 0, 0, 0)),
        out_shape=jax.ShapeDtypeStruct((inputs, count) + own.shape[2:], own.dtype),
        compiler_params=pltpu.CompilerParams(vmem_limit_bytes=VMEM_BYTES),
    )(own)


def unpack_pair(low, high):
    real = jnp.concatenate([low[:, :64], high[:, :64]], axis=1)
    return real, jnp.concatenate([low[:, 64:], high[:, 64:]], axis=1)


def unpacked(ref, channel):
    for p in range(4):
        low = ref[pl.ds(32 * p, 16), channel].reshape(256, 128)
        high = ref[pl.ds(32 * p + 16, 16), channel].reshape(256, 128)
        yield unpack_pair(low, high)


def received(spectra, channels):
    return pl.BlockSpec((spectra.shape[0], channels, 16, 128), lambda c: (0, c, 0, 0))


def unpack_body(ref, out_ref):
    for p, parts in enumerate(unpacked(ref, 0)):
        for n, part in enumerate(parts):
            out_ref[0, n, :, pl.ds(128 * p, 128)] = part


def unpack(spectra):
    channels = spectra.shape[1]
    return pl.pallas_call(
        unpack_body,
        grid=(channels,),
        in_specs=[received(spectra, 1)],
        out_specs=pl.BlockSpec((1, 2, 256, 512), lambda c: (c, 0, 0, 0)),
        out_shape=jax.ShapeDtypeStruct((channels, 2, 256, 512), jnp.bfloat16),
        compiler_params=pltpu.CompilerParams(vmem_limit_bytes=VMEM_BYTES),
        cost_estimate=pl.CostEstimate(
            flops=64 * 1024 * 2048 * 2048, bytes_accessed=9 * 1024 * 1024, transcendentals=0
        ),
    )(spectra)


def correlate_channel(scale, channel, ready_ref, ref, out_ref):
    arrived = [jnp.concatenate(blocks, axis=1) for blocks in zip(*unpacked(ref, channel))]
    r, i = [jnp.concatenate([ready_ref[channel, n], part], axis=0) for n, part in enumerate(arrived)]
    rt, it = r.T, i.T
    both_t, both = jnp.concatenate([rt, it], axis=1), jnp.concatenate([r, i], axis=0)

    def block(left, right, m, n):
        return jnp.dot(
            left[256 * m : 256 * m + 256], right[:, 256 * n : 256 * n + 256], preferred_element_type=jnp.float32
        )

    for m, n in ((0, 0), (0, 1), (1, 1)):
        rows, columns = pl.ds(256 * m, 256), pl.ds(256 * n, 256)
        value = block(both_t, both, m, n) * scale
        cross = block(it, r, m, n) * scale
        out_ref[channel, 0, rows, columns] = value
        if m == n:
            out_ref[channel, 1, rows, columns] = cross - cross.T
        else:
            cross = cross - block(rt, i, m, n) * scale
            out_ref[channel, 0, columns, rows] = value.T
            out_ref[channel, 1, rows, columns] = cross
            out_ref[channel, 1, columns, rows] = -cross.T


def correlate_body(scale, *refs):
    for channel in range(CHANNEL_BLOCK):
        correlate_channel(scale, channel, *refs)


def correlate(first, second, frames):
    channels = second.shape[1]
    return pl.pallas_call(
        functools.partial(correlate_body, 1.0 / frames),
        grid=(channels // CHANNEL_BLOCK,),
        in_specs=[pl.BlockSpec((CHANNEL_BLOCK, 2, 256, 512), lambda c: (c, 0, 0, 0)), received(second, CHANNEL_BLOCK)],
        out_specs=pl.BlockSpec((CHANNEL_BLOCK, 2, 512, 512), lambda c: (c, 0, 0, 0)),
        out_shape=jax.ShapeDtypeStruct((channels, 2, 512, 512), jnp.float32),
        compiler_params=pltpu.CompilerParams(vmem_limit_bytes=VMEM_BYTES),
        cost_estimate=pl.CostEstimate(
            flops=16 * 512 * 512 * 1024, bytes_accessed=25 * 1024 * 1024, transcendentals=0
        ),
    )(first, second)


def per_device(voltages, taps):
    inputs, frames, _, nfft = voltages.shape
    tap_count = taps.shape[0]
    n_tm = lax.axis_size("tm")
    devices = n_tm * lax.axis_size("station")
    after_count = tap_count - 1 - BEFORE

    def blocked(a):
        return a.reshape(a.shape[0], a.shape[1], 2, 8, 128).transpose(0, 1, 3, 2, 4).reshape(a.shape[0], a.shape[1], 16, 128)

    own = blocked(voltages)
    up = [(d, d + 1) for d in range(n_tm - 1)]
    down = [(d, (d - 1) % n_tm) for d in range(n_tm)]
    tail = edge(own, frames // BEFORE - 1, 0, BEFORE)
    before = lax.ppermute(tail, "tm", up)
    head = edge(lax.optimization_barrier((own, tail))[0], 0, 0, after_count)
    after = lax.ppermute(head, "tm", down)
    table = jnp.asarray(transform_rows(nfft))
    keep = (lax.axis_index("tm") < n_tm - 1).astype(jnp.float32).reshape(1)

    wrap = BEFORE + frames
    first, partial = channelize(taps, table, devices, wrap, own=own, keep=keep)
    second = channelize(taps, table, devices, wrap, partial=partial, halo=(before, after))
    first = lax.all_to_all(first, AXES, 0, 0, tiled=True)
    second = lax.all_to_all(second, AXES, 0, 0, tiled=True)
    return correlate(unpack(first), second, n_tm * frames)


def solution(mesh):
    return jax.shard_map(
        per_device,
        mesh=mesh,
        in_specs=(P("station", "tm", None, None), P()),
        out_specs=P(("station", "tm"), None, None, None),
        check_vma=False,
    )
```

```python
import functools
import math

import jax
import jax.numpy as jnp
import ml_dtypes
import numpy as np
from jax import lax
from jax.experimental import pallas as pl
from jax.experimental.pallas import tpu as pltpu
from jax.sharding import PartitionSpec as P

AXES = ("station", "tm")
BEFORE = 8
INNER = tuple(range(23, 31)), tuple(range(31, 39))
OUTER = tuple(range(15, 23)), tuple(range(39, 47))
INPUT_BLOCK = 16
PITCH = TURN = 24
EDGE_STEPS = 2
CHANNEL_BLOCK = 2
VMEM_BYTES = 60 * 1024 * 1024


def transform_rows(nfft):
    channel = np.arange(nfft, dtype=np.int64).reshape(nfft // 4, 4).T
    product = channel[:, :, None] * np.arange(nfft // 4, dtype=np.int64) % nfft
    angle = (np.float32(2.0 * math.pi / nfft) * product.astype(np.float32)).astype(np.float32)
    scale = np.float32(math.sqrt(nfft))
    parts = np.concatenate([np.cos(angle) / scale, np.sin(angle) / scale], axis=2)
    return parts.astype(ml_dtypes.bfloat16)


def filter_terms(outputs, first, last, get, taps_ref, start):
    tap_count = taps_ref.shape[0]
    sums = list(start)
    for e in range(max(first, outputs[0] - tap_count + 1), min(last, outputs[-1] + 1)):
        value = get(e).astype(jnp.float32)
        for n, f in enumerate(outputs):
            if 0 <= f - e < tap_count:
                term = taps_ref[f - e] * value
                sums[n] = term if sums[n] is None else sums[n] + term
    return sums


def filter_own(i, wrap, keep, taps_ref, own_ref, partial_ref, filtered):
    def get(e):
        return own_ref[i, e - BEFORE]

    for g, outputs in enumerate(INNER):
        for n, value in enumerate(filter_terms(outputs, BEFORE, wrap, get, taps_ref, [None] * 8)):
            filtered[8 * g + n, pl.ds(pl.multiple_of(i * PITCH, 8), 16), :] = value
    for g, outputs in enumerate(OUTER):
        for n, value in enumerate(filter_terms(outputs, BEFORE, wrap, get, taps_ref, [None] * 8)):
            partial_ref[i, 8 * g + n] = value if outputs[n] < wrap else value * keep


def filter_halo(i, wrap, taps_ref, partial_ref, before_ref, after_ref, filtered):
    parts = (0, BEFORE, lambda e: before_ref[i, e]), (wrap, wrap + after_ref.shape[1], lambda e: after_ref[i, e - wrap])
    for g, (outputs, (first, last, get)) in enumerate(zip(OUTER, parts)):
        start = [partial_ref[i, 8 * g + n] for n in range(8)]
        for n, value in enumerate(filter_terms(outputs, first, last, get, taps_ref, start)):
            filtered[8 * g + n, pl.ds(pl.multiple_of(i * PITCH, 8), 16), :] = value


def channelize_body(wrap, halo, *refs):
    step = pl.program_id(0)
    rows = INPUT_BLOCK
    if halo:
        taps_ref, table_ref, partial_ref, before_ref, after_ref, out_ref, filtered, data, turned = refs
    else:
        keep_ref, taps_ref, table_ref, own_ref, out_ref, partial_ref, filtered, data, turned = refs

    def filter_input(i, _):
        if halo:
            filter_halo(i, wrap, taps_ref, partial_ref, before_ref, after_ref, filtered)
        else:
            filter_own(i, wrap, keep_ref[0], taps_ref, own_ref, partial_ref, filtered)
        return 0

    lax.fori_loop(0, rows, filter_input, 0)

    def place(f, _):
        at = pl.ds(pl.multiple_of(step * rows, rows), rows)

        def sample(j):
            return [filtered[f, pl.ds(2 * j + part, rows, stride=PITCH), :] for part in range(2)]

        for q in range(2):
            z = [sample(q + 2 * m) for m in range(4)]
            even = [[a + b for a, b in zip(z[m], z[m + 2])] for m in range(2)]
            odd = [[a - b for a, b in zip(z[m], z[m + 2])] for m in range(2)]
            turned_odd = [odd[1][1], -odd[1][0]]
            folded = [
                [a + b for a, b in zip(even[0], even[1])],
                [a + b for a, b in zip(odd[0], turned_odd)],
                [a - b for a, b in zip(even[0], even[1])],
                [a - b for a, b in zip(odd[0], turned_odd)],
            ]
            low, high = pl.ds(q * 128, 128), pl.ds(256 + q * 128, 128)
            for p, (re, im) in enumerate(folded):
                re, im = re.astype(jnp.bfloat16), im.astype(jnp.bfloat16)
                data[p, f, 0, at, low] = re
                data[p, f, 0, at, high] = im
                data[p, f, 1, at, low] = im
                data[p, f, 1, at, high] = -re
        return 0

    lax.fori_loop(0, 16, place, 0)

    @pl.when(step == pl.num_programs(0) - 1)
    def _():
        def transform(n, _):
            for p in range(4):
                pair = data[p, pl.ds(2 * n, 2)].reshape(256, 512)
                result = lax.dot_general(
                    table_ref[p], pair, (((1,), (1,)), ((), ())), preferred_element_type=jnp.float32
                )
                turned[pl.ds(256 * TURN * p + 2 * n, 256, stride=TURN), :] = result[:, :128]
                turned[pl.ds(256 * TURN * p + 2 * n + 1, 256, stride=TURN), :] = result[:, 128:]
            return 0

        lax.fori_loop(0, 8, transform, 0)

        def write(d, _):
            for q in range(2):
                for p in range(4):
                    row = pl.multiple_of(2 * TURN * d, 8) + TURN * (256 * p + q)
                    out_ref[d, 4 * q + p] = turned[pl.ds(row, 16), :].astype(jnp.bfloat16)
            return 0

        lax.fori_loop(0, 128, write, 0, unroll=4)


def channelize(taps, table, devices, wrap, own=None, keep=None, partial=None, halo=()):
    inputs = (partial if own is None else own).shape[0]
    whole = pl.BlockSpec(memory_space=pltpu.VMEM)

    def per_input(shape):
        return pl.BlockSpec((INPUT_BLOCK,) + shape[1:], lambda s: (s, 0, 0, 0))

    sums = jax.ShapeDtypeStruct((inputs, 16, 16, 128), jnp.float32)
    blocks = jax.ShapeDtypeStruct((devices, 8, 16, 128), jnp.bfloat16)
    if own is None:
        operands = [taps, table, partial, *halo]
        specs = [whole, whole] + [per_input(a.shape) for a in operands[2:]]
        out_shape, out_specs = blocks, whole
    else:
        operands = [keep, taps, table, own]
        specs = [pl.BlockSpec(memory_space=pltpu.SMEM), whole, whole, per_input(own.shape)]
        out_shape, out_specs = [blocks, sums], [whole, per_input(sums.shape)]
    return pl.pallas_call(
        functools.partial(channelize_body, wrap, own is None),
        grid=(inputs // INPUT_BLOCK,),
        in_specs=specs,
        out_specs=out_specs,
        out_shape=out_shape,
        scratch_shapes=[
            pltpu.VMEM((16, INPUT_BLOCK * PITCH + 16, 128), jnp.float32),
            pltpu.VMEM((4, 16, 2, 64, 512), jnp.bfloat16),
            pltpu.VMEM((1024 * TURN + 16, 128), jnp.float32),
        ],
        compiler_params=pltpu.CompilerParams(vmem_limit_bytes=VMEM_BYTES),
        cost_estimate=pl.CostEstimate(
            flops=64 * 1024 * 2048 * 2048, bytes_accessed=17 * 1024 * 1024, transcendentals=0
        ),
    )(*operands)


def edge_body(first, source_ref, out_ref):
    out_ref[...] = source_ref[:, first : first + out_ref.shape[1]]


def edge(own, block, first, count):
    inputs = own.shape[0]
    rows = inputs // EDGE_STEPS
    return pl.pallas_call(
        functools.partial(edge_body, first),
        grid=(EDGE_STEPS,),
        in_specs=[pl.BlockSpec((rows, BEFORE) + own.shape[2:], lambda s: (s, block, 0, 0))],
        out_specs=pl.BlockSpec((rows, count) + own.shape[2:], lambda s: (s, 0, 0, 0)),
        out_shape=jax.ShapeDtypeStruct((inputs, count) + own.shape[2:], own.dtype),
        compiler_params=pltpu.CompilerParams(vmem_limit_bytes=VMEM_BYTES),
    )(own)


def unpack_pair(low, high):
    real = jnp.concatenate([low[:, :64], high[:, :64]], axis=1)
    return real, jnp.concatenate([low[:, 64:], high[:, 64:]], axis=1)


def unpacked(ref, channel):
    for p in range(4):
        low = ref[pl.ds(32 * p, 16), channel].reshape(256, 128)
        high = ref[pl.ds(32 * p + 16, 16), channel].reshape(256, 128)
        yield unpack_pair(low, high)


def received(spectra, channels):
    return pl.BlockSpec((spectra.shape[0], channels, 16, 128), lambda c: (0, c, 0, 0))


def unpack_body(ref, out_ref):
    for p, parts in enumerate(unpacked(ref, 0)):
        for n, part in enumerate(parts):
            out_ref[0, n, :, pl.ds(128 * p, 128)] = part


def unpack(spectra):
    channels = spectra.shape[1]
    return pl.pallas_call(
        unpack_body,
        grid=(channels,),
        in_specs=[received(spectra, 1)],
        out_specs=pl.BlockSpec((1, 2, 256, 512), lambda c: (c, 0, 0, 0)),
        out_shape=jax.ShapeDtypeStruct((channels, 2, 256, 512), jnp.bfloat16),
        compiler_params=pltpu.CompilerParams(vmem_limit_bytes=VMEM_BYTES),
        cost_estimate=pl.CostEstimate(
            flops=64 * 1024 * 2048 * 2048, bytes_accessed=9 * 1024 * 1024, transcendentals=0
        ),
    )(spectra)


def correlate_channel(scale, channel, ready_ref, ref, out_ref):
    arrived = [jnp.concatenate(blocks, axis=1) for blocks in zip(*unpacked(ref, channel))]
    r, i = [jnp.concatenate([ready_ref[channel, n], part], axis=0) for n, part in enumerate(arrived)]
    rt, it = r.T, i.T
    both_t, both = jnp.concatenate([rt, it], axis=1), jnp.concatenate([r, i], axis=0)

    def block(left, right, m, n):
        return jnp.dot(
            left[256 * m : 256 * m + 256], right[:, 256 * n : 256 * n + 256], preferred_element_type=jnp.float32
        )

    for m, n in ((0, 0), (0, 1), (1, 1)):
        rows, columns = pl.ds(256 * m, 256), pl.ds(256 * n, 256)
        value = block(both_t, both, m, n) * scale
        cross = block(it, r, m, n) * scale
        out_ref[channel, 0, rows, columns] = value
        if m == n:
            out_ref[channel, 1, rows, columns] = cross - cross.T
        else:
            cross = cross - block(rt, i, m, n) * scale
            out_ref[channel, 0, columns, rows] = value.T
            out_ref[channel, 1, rows, columns] = cross
            out_ref[channel, 1, columns, rows] = -cross.T


def correlate_body(scale, *refs):
    for channel in range(CHANNEL_BLOCK):
        correlate_channel(scale, channel, *refs)


def correlate(first, second, frames):
    channels = second.shape[1]
    return pl.pallas_call(
        functools.partial(correlate_body, 1.0 / frames),
        grid=(channels // CHANNEL_BLOCK,),
        in_specs=[pl.BlockSpec((CHANNEL_BLOCK, 2, 256, 512), lambda c: (c, 0, 0, 0)), received(second, CHANNEL_BLOCK)],
        out_specs=pl.BlockSpec((CHANNEL_BLOCK, 2, 512, 512), lambda c: (c, 0, 0, 0)),
        out_shape=jax.ShapeDtypeStruct((channels, 2, 512, 512), jnp.float32),
        compiler_params=pltpu.CompilerParams(vmem_limit_bytes=VMEM_BYTES),
        cost_estimate=pl.CostEstimate(
            flops=16 * 512 * 512 * 1024, bytes_accessed=25 * 1024 * 1024, transcendentals=0
        ),
    )(first, second)


def per_device(voltages, taps):
    inputs, frames, _, nfft = voltages.shape
    tap_count = taps.shape[0]
    n_tm = lax.axis_size("tm")
    devices = n_tm * lax.axis_size("station")
    after_count = tap_count - 1 - BEFORE

    def blocked(a):
        return a.reshape(a.shape[0], a.shape[1], 2, 8, 128).transpose(0, 1, 3, 2, 4).reshape(a.shape[0], a.shape[1], 16, 128)

    own = blocked(voltages)
    up = [(d, d + 1) for d in range(n_tm - 1)]
    down = [(d, (d - 1) % n_tm) for d in range(n_tm)]
    tail = edge(own, frames // BEFORE - 1, 0, BEFORE)
    before = lax.ppermute(tail, "tm", up)
    head = edge(lax.optimization_barrier((own, tail))[0], 0, 0, after_count)
    after = lax.ppermute(head, "tm", down)
    taps_rows = jnp.repeat(taps.reshape(tap_count, 8, 1, 128), 2, axis=2).reshape(tap_count, 16, 128)
    table = jnp.asarray(transform_rows(nfft))
    keep = (lax.axis_index("tm") < n_tm - 1).astype(jnp.float32).reshape(1)

    wrap = BEFORE + frames
    first, partial = channelize(taps_rows, table, devices, wrap, own=own, keep=keep)
    second = channelize(taps_rows, table, devices, wrap, partial=partial, halo=(before, after))
    first = lax.all_to_all(first, AXES, 0, 0, tiled=True)
    second = lax.all_to_all(second, AXES, 0, 0, tiled=True)
    return correlate(unpack(first), second, n_tm * frames)


def solution(mesh):
    return jax.shard_map(
        per_device,
        mesh=mesh,
        in_specs=(P("station", "tm", None, None), P()),
        out_specs=P(("station", "tm"), None, None, None),
        check_vma=False,
    )
```

```python
import functools
import math

import jax
import jax.numpy as jnp
import ml_dtypes
import numpy as np
from jax import lax
from jax.experimental import pallas as pl
from jax.experimental.pallas import tpu as pltpu
from jax.sharding import PartitionSpec as P

AXES = ("station", "tm")
BEFORE = 8
INNER = tuple(range(23, 31)), tuple(range(31, 39))
OUTER = tuple(range(15, 23)), tuple(range(39, 47))
INPUT_BLOCK = 16
PITCH = TURN = 24
EDGE_STEPS = 2
CHANNEL_BLOCK = 2
VMEM_BYTES = 60 * 1024 * 1024


def transform_rows(nfft):
    channel = np.arange(nfft, dtype=np.int64).reshape(nfft // 4, 4).T
    product = channel[:, :, None] * np.arange(nfft // 4, dtype=np.int64) % nfft
    angle = (np.float32(2.0 * math.pi / nfft) * product.astype(np.float32)).astype(np.float32)
    scale = np.float32(math.sqrt(nfft))
    parts = np.concatenate([np.cos(angle) / scale, np.sin(angle) / scale], axis=2)
    return parts.astype(ml_dtypes.bfloat16)


def filter_terms(outputs, first, last, get, taps_ref, start):
    tap_count = taps_ref.shape[0]
    sums = list(start)
    for e in range(max(first, outputs[0] - tap_count + 1), min(last, outputs[-1] + 1)):
        value = get(e).astype(jnp.float32)
        for n, f in enumerate(outputs):
            if 0 <= f - e < tap_count:
                term = taps_ref[f - e] * value
                sums[n] = term if sums[n] is None else sums[n] + term
    return sums


def filter_own(i, wrap, keep, taps_ref, own_ref, partial_ref, filtered):
    def get(e):
        return own_ref[i, e - BEFORE]

    for g, outputs in enumerate(INNER):
        for n, value in enumerate(filter_terms(outputs, BEFORE, wrap, get, taps_ref, [None] * 8)):
            filtered[8 * g + n, pl.ds(pl.multiple_of(i * PITCH, 8), 16), :] = value
    for g, outputs in enumerate(OUTER):
        for n, value in enumerate(filter_terms(outputs, BEFORE, wrap, get, taps_ref, [None] * 8)):
            partial_ref[i, 8 * g + n] = value if outputs[n] < wrap else value * keep


def filter_halo(i, wrap, taps_ref, partial_ref, before_ref, after_ref, filtered):
    parts = (0, BEFORE, lambda e: before_ref[i, e]), (wrap, wrap + after_ref.shape[1], lambda e: after_ref[i, e - wrap])
    for g, (outputs, (first, last, get)) in enumerate(zip(OUTER, parts)):
        start = [partial_ref[i, 8 * g + n] for n in range(8)]
        for n, value in enumerate(filter_terms(outputs, first, last, get, taps_ref, start)):
            filtered[8 * g + n, pl.ds(pl.multiple_of(i * PITCH, 8), 16), :] = value


def channelize_body(wrap, halo, *refs):
    step = pl.program_id(0)
    rows = INPUT_BLOCK
    if halo:
        taps_ref, table_ref, partial_ref, before_ref, after_ref, out_ref, filtered, data, turned, taps_rows = refs
    else:
        keep_ref, taps_ref, table_ref, own_ref, out_ref, partial_ref, filtered, data, turned, taps_rows = refs

    @pl.when(step == 0)
    def _():
        for j in range(8):
            block = taps_ref[:, 128 * j : 128 * j + 128]
            for part in range(2):
                taps_rows[:, 2 * j + part, :] = block

    def filter_input(i, _):
        if halo:
            filter_halo(i, wrap, taps_rows, partial_ref, before_ref, after_ref, filtered)
        else:
            filter_own(i, wrap, keep_ref[0], taps_rows, own_ref, partial_ref, filtered)
        return 0

    lax.fori_loop(0, rows, filter_input, 0)

    def place(f, _):
        at = pl.ds(pl.multiple_of(step * rows, rows), rows)

        def sample(j):
            return [filtered[f, pl.ds(2 * j + part, rows, stride=PITCH), :] for part in range(2)]

        for q in range(2):
            z = [sample(q + 2 * m) for m in range(4)]
            even = [[a + b for a, b in zip(z[m], z[m + 2])] for m in range(2)]
            odd = [[a - b for a, b in zip(z[m], z[m + 2])] for m in range(2)]
            turned_odd = [odd[1][1], -odd[1][0]]
            folded = [
                [a + b for a, b in zip(even[0], even[1])],
                [a + b for a, b in zip(odd[0], turned_odd)],
                [a - b for a, b in zip(even[0], even[1])],
                [a - b for a, b in zip(odd[0], turned_odd)],
            ]
            low, high = pl.ds(q * 128, 128), pl.ds(256 + q * 128, 128)
            for p, (re, im) in enumerate(folded):
                re, im = re.astype(jnp.bfloat16), im.astype(jnp.bfloat16)
                data[p, f, 0, at, low] = re
                data[p, f, 0, at, high] = im
                data[p, f, 1, at, low] = im
                data[p, f, 1, at, high] = -re
        return 0

    lax.fori_loop(0, 16, place, 0)

    @pl.when(step == pl.num_programs(0) - 1)
    def _():
        def transform(n, _):
            for p in range(4):
                pair = data[p, pl.ds(2 * n, 2)].reshape(256, 512)
                result = lax.dot_general(
                    table_ref[p], pair, (((1,), (1,)), ((), ())), preferred_element_type=jnp.float32
                )
                turned[pl.ds(256 * TURN * p + 2 * n, 256, stride=TURN), :] = result[:, :128]
                turned[pl.ds(256 * TURN * p + 2 * n + 1, 256, stride=TURN), :] = result[:, 128:]
            return 0

        lax.fori_loop(0, 8, transform, 0, unroll=2 if halo else 1)

        def write(d, _):
            for q in range(2):
                for p in range(4):
                    row = pl.multiple_of(2 * TURN * d, 8) + TURN * (256 * p + q)
                    out_ref[d, 4 * q + p] = turned[pl.ds(row, 16), :].astype(jnp.bfloat16)
            return 0

        lax.fori_loop(0, 128, write, 0, unroll=4)


def channelize(taps, table, devices, wrap, own=None, keep=None, partial=None, halo=()):
    inputs = (partial if own is None else own).shape[0]
    whole = pl.BlockSpec(memory_space=pltpu.VMEM)

    def per_input(shape):
        return pl.BlockSpec((INPUT_BLOCK,) + shape[1:], lambda s: (s, 0, 0, 0))

    sums = jax.ShapeDtypeStruct((inputs, 16, 16, 128), jnp.float32)
    blocks = jax.ShapeDtypeStruct((devices, 8, 16, 128), jnp.bfloat16)
    if own is None:
        operands = [taps, table, partial, *halo]
        specs = [whole, whole] + [per_input(a.shape) for a in operands[2:]]
        out_shape, out_specs = blocks, whole
    else:
        operands = [keep, taps, table, own]
        specs = [pl.BlockSpec(memory_space=pltpu.SMEM), whole, whole, per_input(own.shape)]
        out_shape, out_specs = [blocks, sums], [whole, per_input(sums.shape)]
    return pl.pallas_call(
        functools.partial(channelize_body, wrap, own is None),
        grid=(inputs // INPUT_BLOCK,),
        in_specs=specs,
        out_specs=out_specs,
        out_shape=out_shape,
        scratch_shapes=[
            pltpu.VMEM((16, INPUT_BLOCK * PITCH + 16, 128), jnp.float32),
            pltpu.VMEM((4, 16, 2, 64, 512), jnp.bfloat16),
            pltpu.VMEM((1024 * TURN + 16, 128), jnp.float32),
            pltpu.VMEM((taps.shape[0], 16, 128), jnp.float32),
        ],
        compiler_params=pltpu.CompilerParams(vmem_limit_bytes=VMEM_BYTES),
        cost_estimate=pl.CostEstimate(
            flops=64 * 1024 * 2048 * 2048, bytes_accessed=17 * 1024 * 1024, transcendentals=0
        ),
    )(*operands)


def edge_body(first, source_ref, out_ref):
    out_ref[...] = source_ref[:, first : first + out_ref.shape[1]]


def edge(own, block, first, count):
    inputs = own.shape[0]
    rows = inputs // EDGE_STEPS
    return pl.pallas_call(
        functools.partial(edge_body, first),
        grid=(EDGE_STEPS,),
        in_specs=[pl.BlockSpec((rows, BEFORE) + own.shape[2:], lambda s: (s, block, 0, 0))],
        out_specs=pl.BlockSpec((rows, count) + own.shape[2:], lambda s: (s, 0, 0, 0)),
        out_shape=jax.ShapeDtypeStruct((inputs, count) + own.shape[2:], own.dtype),
        compiler_params=pltpu.CompilerParams(vmem_limit_bytes=VMEM_BYTES),
    )(own)


def unpack_pair(low, high):
    real = jnp.concatenate([low[:, :64], high[:, :64]], axis=1)
    return real, jnp.concatenate([low[:, 64:], high[:, 64:]], axis=1)


def unpacked(ref, channel):
    for p in range(4):
        low = ref[pl.ds(32 * p, 16), channel].reshape(256, 128)
        high = ref[pl.ds(32 * p + 16, 16), channel].reshape(256, 128)
        yield unpack_pair(low, high)


def received(spectra, channels):
    return pl.BlockSpec((spectra.shape[0], channels, 16, 128), lambda c: (0, c, 0, 0))


def unpack_body(ref, out_ref):
    for p, parts in enumerate(unpacked(ref, 0)):
        for n, part in enumerate(parts):
            out_ref[0, n, :, pl.ds(128 * p, 128)] = part


def unpack(spectra):
    channels = spectra.shape[1]
    return pl.pallas_call(
        unpack_body,
        grid=(channels,),
        in_specs=[received(spectra, 1)],
        out_specs=pl.BlockSpec((1, 2, 256, 512), lambda c: (c, 0, 0, 0)),
        out_shape=jax.ShapeDtypeStruct((channels, 2, 256, 512), jnp.bfloat16),
        compiler_params=pltpu.CompilerParams(vmem_limit_bytes=VMEM_BYTES),
        cost_estimate=pl.CostEstimate(
            flops=64 * 1024 * 2048 * 2048, bytes_accessed=9 * 1024 * 1024, transcendentals=0
        ),
    )(spectra)


def correlate_channel(scale, channel, ready_ref, ref, out_ref):
    arrived = [jnp.concatenate(blocks, axis=1) for blocks in zip(*unpacked(ref, channel))]
    r, i = [jnp.concatenate([ready_ref[channel, n], part], axis=0) for n, part in enumerate(arrived)]
    rt, it = r.T, i.T
    both_t, both = jnp.concatenate([rt, it], axis=1), jnp.concatenate([r, i], axis=0)

    def block(left, right, m, n):
        return jnp.dot(
            left[256 * m : 256 * m + 256], right[:, 256 * n : 256 * n + 256], preferred_element_type=jnp.float32
        )

    for m, n in ((0, 0), (0, 1), (1, 1)):
        rows, columns = pl.ds(256 * m, 256), pl.ds(256 * n, 256)
        value = block(both_t, both, m, n) * scale
        cross = block(it, r, m, n) * scale
        out_ref[channel, 0, rows, columns] = value
        if m == n:
            out_ref[channel, 1, rows, columns] = cross - cross.T
        else:
            cross = cross - block(rt, i, m, n) * scale
            out_ref[channel, 0, columns, rows] = value.T
            out_ref[channel, 1, rows, columns] = cross
            out_ref[channel, 1, columns, rows] = -cross.T


def correlate_body(scale, *refs):
    for channel in range(CHANNEL_BLOCK):
        correlate_channel(scale, channel, *refs)


def correlate(first, second, frames):
    channels = second.shape[1]
    return pl.pallas_call(
        functools.partial(correlate_body, 1.0 / frames),
        grid=(channels // CHANNEL_BLOCK,),
        in_specs=[pl.BlockSpec((CHANNEL_BLOCK, 2, 256, 512), lambda c: (c, 0, 0, 0)), received(second, CHANNEL_BLOCK)],
        out_specs=pl.BlockSpec((CHANNEL_BLOCK, 2, 512, 512), lambda c: (c, 0, 0, 0)),
        out_shape=jax.ShapeDtypeStruct((channels, 2, 512, 512), jnp.float32),
        compiler_params=pltpu.CompilerParams(vmem_limit_bytes=VMEM_BYTES),
        cost_estimate=pl.CostEstimate(
            flops=16 * 512 * 512 * 1024, bytes_accessed=25 * 1024 * 1024, transcendentals=0
        ),
    )(first, second)


def per_device(voltages, taps):
    inputs, frames, _, nfft = voltages.shape
    tap_count = taps.shape[0]
    n_tm = lax.axis_size("tm")
    devices = n_tm * lax.axis_size("station")
    after_count = tap_count - 1 - BEFORE

    def blocked(a):
        return a.reshape(a.shape[0], a.shape[1], 2, 8, 128).transpose(0, 1, 3, 2, 4).reshape(a.shape[0], a.shape[1], 16, 128)

    own = blocked(voltages)
    up = [(d, d + 1) for d in range(n_tm - 1)]
    down = [(d, (d - 1) % n_tm) for d in range(n_tm)]
    tail = edge(own, frames // BEFORE - 1, 0, BEFORE)
    before = lax.ppermute(tail, "tm", up)
    head = edge(lax.optimization_barrier((own, tail))[0], 0, 0, after_count)
    after = lax.ppermute(head, "tm", down)
    table = jnp.asarray(transform_rows(nfft))
    keep = (lax.axis_index("tm") < n_tm - 1).astype(jnp.float32).reshape(1)

    wrap = BEFORE + frames
    first, partial = channelize(taps, table, devices, wrap, own=own, keep=keep)
    second = channelize(taps, table, devices, wrap, partial=partial, halo=(before, after))
    first = lax.all_to_all(first, AXES, 0, 0, tiled=True)
    second = lax.all_to_all(second, AXES, 0, 0, tiled=True)
    return correlate(unpack(first), second, n_tm * frames)


def solution(mesh):
    return jax.shard_map(
        per_device,
        mesh=mesh,
        in_specs=(P("station", "tm", None, None), P()),
        out_specs=P(("station", "tm"), None, None, None),
        check_vma=False,
    )
```
